32 devices in a mesh: groups: 2 (over x), row: 16 (over z, y, core).
Axes of the slice: x: 2, y: 2, z: 4, core: 2. Of those that a mesh axis runs over, the one named last changes fastest.
Arguments:
- t2_panels: bfloat16 [32, 1024, 1280], P(('groups', 'row')), parts along dimension 0, may hold values from -6 to 6
- t2_mask: int32 [32, 4, 5], P(('groups', 'row')), parts along dimension 0, may hold values from 0 to 1, as said below
- v_blocks: bfloat16 [4, 1280, 32768], P('groups', None, 'row'), parts along dimension 0, may hold values from -0.1875 to 0.1875
- v_mask: int32 [4, 5, 128], P('groups', None, 'row'), parts along dimension 0, may hold values 0 or 1
- r_mask: int32 [8, 128], P('groups', 'row'), parts along dimension 0, may hold values 0 or 1
- owner_map: int32 [256, 4, 1], P(('groups', 'row')), parts along dimension 0, may hold values from 0 to 15; in each aligned block of 32 rows (0 to 31, 32 to 63, ..., all dimensions but the last counted through in order) at most 4 rows name the same one
- section_owner: int32 [4], P('groups'), parts along dimension 0, may hold values from 0 to 15
Outputs:
- delivered: bfloat16 [512, 4, 256, 256], P(('groups', 'row')), parts along dimension 0
The draws below stay inside these ranges and needn't reach their ends.
There are 2 independent parts, one for each index of `groups`. The reference program is written for one: setup_inputs(seed, part) draws one part's arguments, and reference() takes and returns one part's arrays. A program takes and returns all parts, laid end to end along the dimension named above; each array names one. Nothing has to cross between parts.
Inputs may be any that keep to these rules, and one draw needn't show every extreme that they name: `t2_mask`: each device's panel has exactly 10 tiles of ones. `owner_map`: among the 32 tiles of one device no owner appears more than 4 times.
All inputs are finite; a program needn't handle non-finite values. No bound on the sum of `v_mask` or of `r_mask` on one device may be relied on, other than what follows from the above.
Results may differ from the reference program's by a relative error of at most 0.001.
Values may be sent and summed in bfloat16 or wider, within the bound.
No kernel may reach another device: no remote copies, remote signals or barrier semaphores. Data moves between devices by JAX's collectives and lax.ppermute only.
A program may use at most 192 MiB of HBM per device.

```python
import math
import jax
import jax.numpy as jnp
import numpy as np
from jax import lax

TILE = 256
MT = 4
KPT = 5
NT_DEV = 8
SECTIONS = 2
PCAP = 10
CAP = 4
NT = 128
N_ROW = 16


def draw_t2_mask(key, part):
    key = jax.random.fold_in(key, 11)
    keys = jax.random.split(key, N_ROW)
    orders = jax.vmap(lambda sub_key: jax.random.permutation(sub_key, MT * KPT))(keys)
    return (orders < PCAP).astype(jnp.int32).reshape(N_ROW, MT, KPT)


def set_ends(array, rng, smallest, largest):
    place = [jax.random.randint(jax.random.fold_in(rng, axis), (), 0, length) for axis, length in enumerate(array.shape)]
    widest = array.shape.index(max(array.shape))
    neighbour = place[:widest] + [(place[widest] + 1) % array.shape[widest]] + place[widest + 1:]
    return array.at[tuple(place)].set(smallest).at[tuple(neighbour)].set(largest)


def levels(key, dims, cuts, smallest, largest):
    level = 1.0
    for dim, blocks in cuts:
        draws = jax.random.uniform(jax.random.fold_in(jax.random.fold_in(key, 6), dim), (blocks,), jnp.float32, smallest / len(cuts), largest / len(cuts))
        level = level * jnp.repeat(jnp.exp(draws), dims[dim] // blocks).reshape((-1,) + (1,) * (len(dims) - 1 - dim))
    return level


def deal_out(rng, own, number, rows, count, top, bound, lean):
    order = jax.random.permutation(rng, count)
    crowded, common = load_shares(count, rows * top, bound, lean, True), load_shares(count, rows * top, bound, lean, False)
    places = jnp.arange(count)

    def named(lengths, offset_by):
        used = int((lengths > 0).sum())
        fixed = max(1, used // 4)
        shifted = fixed + (places - fixed + offset_by * (used - fixed)) % max(1, count - fixed)
        return jnp.zeros((count,), jnp.int32).at[order[jnp.where(places < fixed, places, shifted)]].set(jnp.asarray(lengths, jnp.int32))

    lengths = jnp.where(number % 4 == 0, named(crowded, number // 4), named(common, number - number // 4 - 1))
    mixed = jax.random.permutation(jax.random.fold_in(own, 3), count)
    source_of, receiver = mixed[0:count // 2 * 2:2], mixed[1:count // 2 * 2:2]
    slack = jnp.minimum(lengths[source_of] - 1, bound - lengths[receiver]) // 2
    slack = jnp.where((source_of == order[0]) | (receiver == order[0]) | (lengths[receiver] == 0), 0, jnp.maximum(slack, 0))
    shifted = jax.random.randint(jax.random.fold_in(own, 4), (count // 2,), 0, 1 << 20) % (slack + 1)
    lengths = lengths.at[source_of].add(-shifted).at[receiver].add(shifted)
    labels = jnp.searchsorted(jnp.cumsum(lengths), jnp.arange(rows * top), side="right").astype(jnp.int32)
    table = labels.reshape(top, rows).T
    table = table[jax.random.permutation(jax.random.fold_in(own, 1), rows)]
    offset_by = jax.random.randint(jax.random.fold_in(own, 2), (rows, 1), 0, top)
    return jnp.take_along_axis(table, (jnp.arange(top)[None, :] + offset_by) % top, axis=1)


def load_shares(number_of, total, reach, lean, full):
    weights = [(1 << 20) // math.isqrt(standing ** lean) + 1 for standing in range(1, number_of + 1)]
    largest = reach if full else min(reach, max(-(-total // number_of), total * weights[0] // sum(weights)))
    least = 1 if total - largest >= number_of - 1 else 0
    given, rest = [largest] + [least] * (number_of - 1), total - largest - least * (number_of - 1)
    while rest > 0:
        movable = [i for i in range(1, number_of) if given[i] < largest] or [i for i in range(1, number_of) if given[i] < reach]
        whole, budget = sum([weights[i] for i in movable]), rest
        for i in movable:
            addition = min(reach - given[i], max(1, budget * weights[i] // whole), rest)
            given[i] = given[i] + addition
            rest = rest - addition
    return np.array(given)


def gaussian(key, dims, deviation, reach, shards=(), kind=jnp.bfloat16):
    values = deviation * jax.random.normal(key, dims, jnp.float32)
    if shards:
        values = values * levels(key, dims, shards, -0.22, 0.18)
    return jnp.clip(values, -reach, reach).astype(kind)


def setup_inputs(seed: int = 0, part: int = 0) -> dict:
    key_of = jax.random.split(jax.random.key(seed), 8)
    part_splits = jax.random.split(jax.random.fold_in(key_of[7], part), 8)
    t2_panels = gaussian(part_splits[0], (N_ROW, MT * TILE, KPT * TILE), 1.0, 6.0, ((0, 16),))
    t2_mask = draw_t2_mask(jax.random.fold_in(jax.random.fold_in(key_of[7], part), 71), part)
    v_blocks = gaussian(part_splits[2], (SECTIONS, KPT * TILE, NT * TILE), (3 * SECTIONS * KPT * TILE // 8) ** -0.5, 0.1875, ((2, 16),))
    v_mask = set_ends((jax.random.randint(part_splits[3], (SECTIONS, KPT, NT), 0, 4) < 3).astype(jnp.int32), jax.random.fold_in(part_splits[3], 1), 0, 1)
    r_mask = set_ends((jax.random.randint(part_splits[4], (MT, NT), 0, 4) < 3).astype(jnp.int32), jax.random.fold_in(part_splits[4], 1), 0, 1)
    owner_map_keys = jax.random.split(jax.random.fold_in(part_splits[5], 1), NT * MT // (MT * NT_DEV))
    owner_map_turns = jax.random.permutation(jax.random.fold_in(part_splits[5], 3), NT * MT // (MT * NT_DEV))
    owner_map = jax.vmap(lambda own, number: deal_out(jax.random.fold_in(part_splits[5], 2), own, number, MT * NT_DEV, N_ROW, 1, CAP, 2))(owner_map_keys, owner_map_turns).reshape((NT, MT, 1))
    section_owner = jax.random.randint(part_splits[6], (SECTIONS,), 0, N_ROW).astype(jnp.int32)
    return dict(t2_panels=t2_panels, t2_mask=t2_mask, v_blocks=v_blocks, v_mask=v_mask, r_mask=r_mask, owner_map=owner_map, section_owner=section_owner)


def reference(t2_panels, t2_mask, v_blocks, v_mask, r_mask, owner_map, section_owner):
    ranks = N_ROW
    tile_count = MT * NT_DEV
    expand = t2_mask.astype(t2_panels.dtype)[:, :, None, :, None]
    masked_all = (t2_panels.reshape(ranks, MT, TILE, KPT, TILE) * expand).reshape(ranks, MT * TILE, KPT * TILE)
    amplitude = masked_all[section_owner].astype(jnp.float32)
    owner_range = jnp.arange(ranks, dtype=jnp.int32)

    def per_source(device_index):
        first = device_index * NT_DEV
        v_part = lax.dynamic_slice_in_dim(v_blocks, first * TILE, NT_DEV * TILE, 2)
        vm_part = lax.dynamic_slice_in_dim(v_mask, first, NT_DEV, 2)
        masked_v = (v_part.reshape(SECTIONS, KPT, TILE, NT_DEV, TILE) * vm_part.astype(v_part.dtype)[:, :, None, :, None]).reshape(SECTIONS, KPT * TILE, NT_DEV * TILE)
        total = jnp.zeros((MT * TILE, NT_DEV * TILE), jnp.float32)
        for section_index in range(SECTIONS):
            total = total + jnp.dot(amplitude[section_index], masked_v[section_index].astype(jnp.float32), precision=lax.Precision.HIGHEST)
        rm_part = lax.dynamic_slice_in_dim(r_mask, first, NT_DEV, 1).astype(jnp.float32)
        result = (total.reshape(MT, TILE, NT_DEV, TILE) * rm_part[:, None, :, None]).astype(jnp.bfloat16)
        tiles = result.transpose(2, 0, 1, 3).reshape(tile_count, TILE, TILE)
        target = lax.dynamic_slice_in_dim(owner_map, first, NT_DEV, 0).reshape(tile_count).astype(jnp.int32)
        onehot = (target[:, None] == owner_range[None, :]).astype(jnp.int32)
        before = jnp.cumsum(onehot, axis=0) - onehot
        rank_of = jnp.sum(before * onehot, axis=1).astype(jnp.int32)
        slot = target * CAP + rank_of
        sending = jnp.zeros((ranks * CAP, TILE, TILE), jnp.bfloat16).at[slot].set(tiles)
        return sending.reshape(ranks, CAP, TILE, TILE)

    sends = lax.map(per_source, jnp.arange(ranks, dtype=jnp.int32))
    return sends.transpose(1, 0, 2, 3, 4).reshape(ranks * ranks, CAP, TILE, TILE)
```

```python
import functools

import jax
import jax.numpy as jnp
from jax import lax
from jax.experimental import pallas as pl
from jax.experimental.pallas import tpu as pltpu
from jax.sharding import PartitionSpec as P

TILE = 256
MT = 4
KPT = 5
NT_DEV = 8
SECTIONS = 2
PCAP = 10
TILES = MT * NT_DEV
SPILL = 3
STEP_TILES = 2
STEP_COLS = STEP_TILES * TILE
ANY = pl.BlockSpec(memory_space=pl.ANY)
SMEM = pl.BlockSpec(memory_space=pltpu.SMEM)
VMEM = pl.BlockSpec(memory_space=pltpu.VMEM)


def swap(x, bit, ranks):
    return lax.ppermute(x, "row", [(i, i ^ bit) for i in range(ranks)])


def scatter_step(x, me, roots, bit, ranks):
    half = x.shape[1] // 2
    high = (me & bit) != 0
    low_rows, high_rows = x[:, :half], x[:, half:]
    own = jnp.where(high, high_rows, low_rows)
    got = swap(jnp.where(high, low_rows, high_rows), bit, ranks)
    return jnp.where((((me ^ roots) & bit) == 0)[:, None, None], own, got)


def middle_step(x, me, roots, bit, ranks):
    got = swap(x, bit, ranks)
    return jnp.where((((me ^ roots) & bit) == 0)[:, None, None], x, got)


def gather_step(x, me, bit, ranks):
    got = swap(x, bit, ranks)
    high = (me & bit) != 0
    return jnp.concatenate([jnp.where(high, got, x), jnp.where(high, x, got)], axis=1)


def spread(x, me, roots, ranks):
    x = scatter_step(x, me, roots, 1, ranks)
    half = x.shape[1] // 2
    a, b = x[:, :half], x[:, half:]
    a, b = scatter_step(a, me, roots, 2, ranks), scatter_step(b, me, roots, 4, ranks)
    a, b = scatter_step(a, me, roots, 4, ranks), scatter_step(b, me, roots, 2, ranks)
    bit = 8
    while bit < ranks:
        a, b = middle_step(a, me, roots, bit, ranks), middle_step(b, me, roots, bit, ranks)
        bit *= 2
    a, b = gather_step(a, me, 4, ranks), gather_step(b, me, 2, ranks)
    a, b = gather_step(a, me, 2, ranks), gather_step(b, me, 4, ranks)
    return gather_step(jnp.concatenate([a, b], axis=1), me, 1, ranks)


def gather_table(x, me, ranks):
    bit = 1
    while bit < ranks:
        got = swap(x, bit, ranks)
        high = (me & bit) != 0
        x = jnp.concatenate([jnp.where(high, got, x), jnp.where(high, x, got)], axis=0)
        bit *= 2
    return x


def nonzero_tiles(mask):
    ones = (mask != 0).astype(jnp.int32)
    places = jnp.arange(MT * KPT, dtype=jnp.int32)
    earlier = (places[None, :] < places[:, None]).astype(jnp.int32)
    before = jnp.sum(ones[..., None, :] * earlier, axis=-1)
    hit = ones[..., None, :] * (before[..., None, :] == jnp.arange(PCAP)[:, None])
    return jnp.sum(hit * places, axis=-1)


def ranks_of(owners, keep, direct):
    order = jnp.arange(TILES)
    earlier = order[None, :] < order[:, None]
    same = (owners[:, :, None] == owners[:, None, :]) & earlier
    rank = jnp.sum(same, axis=2, dtype=jnp.int32)
    kept_rank = jnp.sum(same & keep[:, None, :], axis=2, dtype=jnp.int32)
    spills = keep & (kept_rank >= direct)
    spill_place = jnp.sum(spills[:, None, :] & earlier, axis=2, dtype=jnp.int32)
    return rank, kept_rank, spills, spill_place


def pack_kernel(tile_ref, panel_ref, out_ref, sem):
    copies = []
    for i in range(PCAP):
        place = tile_ref[i]
        m, k = place // KPT, lax.rem(place, KPT)
        copies.append(
            pltpu.make_async_copy(
                panel_ref.at[
                    pl.ds(pl.multiple_of(m * TILE, TILE), TILE), pl.ds(pl.multiple_of(k * TILE, TILE), TILE)
                ],
                out_ref.at[pl.ds(i * TILE, TILE)],
                sem.at[i],
            )
        )
    for copy in copies:
        copy.start()
    for copy in copies:
        copy.wait()


def pack(panel, tiles):
    return pl.pallas_call(
        pack_kernel,
        out_shape=jax.ShapeDtypeStruct((PCAP * TILE, TILE), jnp.bfloat16),
        in_specs=[SMEM, ANY],
        out_specs=ANY,
        scratch_shapes=[pltpu.SemaphoreType.DMA((PCAP,))],
        name="pack_panel",
    )(tiles, panel)


def ladder_kernel(split, tile_ref, place_ref, amp_ref, v_ref, mask_ref, out_ref, spill_ref, acc, staged, sem):
    step = pl.program_id(0)
    acc[...] = jnp.zeros_like(acc)
    for s in range(SECTIONS):
        for i in range(PCAP):
            place = tile_ref[s * PCAP + i]
            m, k = place // KPT, lax.rem(place, KPT)
            masked = v_ref[s, pl.ds(pl.multiple_of(k * TILE, TILE), TILE), :] * mask_ref[s, k]
            acc[m] += jnp.dot(
                amp_ref[s, i * TILE : (i + 1) * TILE, :], masked, preferred_element_type=jnp.float32
            )

    def copy_to(q, ref, place):
        return pltpu.make_async_copy(staged.at[q], ref.at[place], sem.at[q])

    for j in range(STEP_TILES):
        for m in range(MT):
            q = (step * STEP_TILES + j) * MT + m
            staged[q] = acc[m, :, j * TILE : (j + 1) * TILE].astype(jnp.bfloat16)
            place = place_ref[q]

            @pl.when((place >= 0) & (place < split))
            def _():
                copy_to(q, out_ref, place).start()

            @pl.when(place >= split)
            def _():
                copy_to(q, spill_ref, place - split).start()

    @pl.when(step == NT_DEV // STEP_TILES - 1)
    def _():
        def finish(q, carry):
            @pl.when(place_ref[q] >= 0)
            def _():
                copy_to(q, out_ref, 0).wait()

            return carry

        lax.fori_loop(0, TILES, finish, 0)


def ladder(amp, amp_tiles, v_blocks, v_rows, places, split):
    return pl.pallas_call(
        functools.partial(ladder_kernel, split),
        out_shape=(
            jax.ShapeDtypeStruct((split, TILE, TILE), jnp.bfloat16),
            jax.ShapeDtypeStruct((SPILL, TILE, TILE), jnp.bfloat16),
        ),
        grid=(NT_DEV // STEP_TILES,),
        in_specs=[
            SMEM,
            SMEM,
            VMEM,
            pl.BlockSpec((SECTIONS, KPT * TILE, STEP_COLS), lambda j: (0, 0, j)),
            pl.BlockSpec((SECTIONS, KPT, 1, STEP_COLS), lambda j: (0, 0, 0, j)),
        ],
        out_specs=(ANY, ANY),
        scratch_shapes=[
            pltpu.VMEM((MT, TILE, STEP_COLS), jnp.float32),
            pltpu.VMEM((TILES, TILE, TILE), jnp.bfloat16),
            pltpu.SemaphoreType.DMA((TILES,)),
        ],
        compiler_params=pltpu.CompilerParams(vmem_limit_bytes=48 * 1024 * 1024),
        name="ladder",
    )(amp_tiles, places, amp, v_blocks, v_rows)


def place_kernel(slots, split, table_ref, direct_ref, spill_ref, out_ref, zero, sem):
    zero[...] = jnp.zeros_like(zero)

    def begin(j, carry):
        source = table_ref[j]

        @pl.when(source < 0)
        def _():
            pltpu.make_async_copy(zero, out_ref.at[j], sem.at[j]).start()

        @pl.when((source >= 0) & (source < split))
        def _():
            pltpu.make_async_copy(direct_ref.at[source], out_ref.at[j], sem.at[j]).start()

        @pl.when(source >= split)
        def _():
            pltpu.make_async_copy(spill_ref.at[source - split], out_ref.at[j], sem.at[j]).start()

        return carry

    def finish(j, carry):
        pltpu.make_async_copy(zero, out_ref.at[j], sem.at[j]).wait()
        return carry

    lax.fori_loop(0, slots, begin, 0)
    lax.fori_loop(0, slots, finish, 0)


def place_tiles(table, direct, spill):
    slots, split = table.shape[0], direct.shape[0]
    return pl.pallas_call(
        functools.partial(place_kernel, slots, split),
        out_shape=jax.ShapeDtypeStruct((slots, TILE, TILE), jnp.bfloat16),
        in_specs=[SMEM, ANY, ANY],
        out_specs=ANY,
        scratch_shapes=[pltpu.VMEM((TILE, TILE), jnp.bfloat16), pltpu.SemaphoreType.DMA((slots,))],
        name="place_tiles",
    )(table, direct, spill)


def exchange(tiles, ranks):
    count = tiles.shape[0] // ranks
    sent = tiles.reshape(ranks, count, TILE, TILE)
    return lax.all_to_all(sent, "row", split_axis=0, concat_axis=0, tiled=True).reshape(
        ranks * count, TILE, TILE
    )


def local(t2_panels, t2_mask, v_blocks, v_mask, r_mask, owner_map, section_owner):
    ranks, groups = lax.axis_size("row"), lax.axis_size("groups")
    me = lax.axis_index("row")
    slots_each = max(2, 2 * TILES // ranks)
    direct = slots_each // 2
    roots = section_owner

    packed = pack(t2_panels[0], nonzero_tiles(t2_mask.reshape(MT * KPT)))
    amp = spread(
        jnp.broadcast_to(packed[None], (SECTIONS,) + packed.shape), me, roots, ranks
    )

    own_code = owner_map.reshape(1, TILES) * 2 + (r_mask.T.reshape(1, TILES) != 0).astype(jnp.int32)
    codes = gather_table(
        jnp.concatenate([own_code, t2_mask.reshape(1, MT * KPT)], axis=1), me, ranks
    )
    owners, keep = codes[:, :TILES] // 2, codes[:, :TILES] % 2 != 0
    amp_tiles = nonzero_tiles(jnp.take(codes[:, TILES:], roots, axis=0)).reshape(-1)
    rank, kept_rank, spills, spill_place = ranks_of(owners, keep, direct)
    most = jnp.max(jnp.sum(spills, axis=1, dtype=jnp.int32)).reshape(1, 1)
    worst = most
    for turn in range(1, groups):
        worst = jnp.maximum(
            worst, lax.ppermute(most, "groups", [(g, (g + turn) % groups) for g in range(groups)])
        )

    device = jnp.arange(ranks, dtype=jnp.int32)[:, None]
    slot = jnp.arange(slots_each, dtype=jnp.int32)
    arrives = ((owners == me) & keep)[:, None, :] & (rank[:, None, :] == slot[None, :, None])

    def row_of(x):
        return lax.dynamic_index_in_dim(x, me, 0, keepdims=False)

    def table_of(origin):
        return (jnp.sum(jnp.where(arrives, origin[:, None, :] + 1, 0), axis=2) - 1).reshape(-1)

    v_rows = jnp.repeat(v_mask.astype(jnp.bfloat16), TILE, axis=2)[:, :, None, :]

    split = ranks * direct
    short_places = row_of(
        jnp.where(keep, jnp.where(spills, split + spill_place, owners * direct + kept_rank), -1)
    )
    short_table = table_of(
        jnp.where(spills, split + device * SPILL + spill_place, device * direct + kept_rank)
    )
    long_places = row_of(jnp.where(keep, owners * slots_each + kept_rank, -1))
    long_table = table_of(device * slots_each + kept_rank)

    def short(amp, v_blocks):
        tiles, spill = ladder(amp, amp_tiles, v_blocks, v_rows, short_places, split)
        gathered = lax.all_gather(spill, "row", axis=0, tiled=True)
        return place_tiles(short_table, exchange(tiles, ranks), gathered)

    def long(amp, v_blocks):
        tiles, spill = ladder(amp, amp_tiles, v_blocks, v_rows, long_places, ranks * slots_each)
        return place_tiles(long_table, exchange(tiles, ranks), spill)

    delivered = lax.cond(worst[0, 0] <= SPILL, short, long, amp, v_blocks)
    return delivered.reshape(ranks, slots_each, TILE, TILE)


def solution(mesh):
    placed = (
        P(("groups", "row"), None, None),
        P(("groups", "row"), None, None),
        P("groups", None, "row"),
        P("groups", None, "row"),
        P("groups", "row"),
        P(("groups", "row"), None, None),
        P("groups"),
    )
    return jax.shard_map(
        local,
        mesh=mesh,
        in_specs=placed,
        out_specs=P(("groups", "row"), None, None, None),
        check_vma=False,
    )
```

```python
import functools

import jax
import jax.numpy as jnp
from jax import lax
from jax.experimental import pallas as pl
from jax.experimental.pallas import tpu as pltpu
from jax.sharding import PartitionSpec as P

TILE = 256
MT = 4
KPT = 5
NT_DEV = 8
SECTIONS = 2
PCAP = 10
TILES = MT * NT_DEV
SPILL = 3
STEP_TILES = 2
STEP_COLS = STEP_TILES * TILE
ANY = pl.BlockSpec(memory_space=pl.ANY)
SMEM = pl.BlockSpec(memory_space=pltpu.SMEM)
VMEM = pl.BlockSpec(memory_space=pltpu.VMEM)


def swap(x, bit, ranks):
    return lax.ppermute(x, "row", [(i, i ^ bit) for i in range(ranks)])


def scatter_step(x, me, roots, bit, ranks):
    half = x.shape[1] // 2
    high = (me & bit) != 0
    low_rows, high_rows = x[:, :half], x[:, half:]
    own = jnp.where(high, high_rows, low_rows)
    got = swap(jnp.where(high, low_rows, high_rows), bit, ranks)
    return jnp.where((((me ^ roots) & bit) == 0)[:, None, None], own, got)


def middle_step(x, me, roots, bit, ranks):
    got = swap(x, bit, ranks)
    return jnp.where((((me ^ roots) & bit) == 0)[:, None, None], x, got)


def gather_step(x, me, bit, ranks):
    got = swap(x, bit, ranks)
    high = (me & bit) != 0
    return jnp.concatenate([jnp.where(high, got, x), jnp.where(high, x, got)], axis=1)


def spread(x, me, roots, ranks):
    x = scatter_step(x, me, roots, 1, ranks)
    half = x.shape[1] // 2
    a, b = x[:, :half], x[:, half:]
    a, b = scatter_step(a, me, roots, 2, ranks), scatter_step(b, me, roots, 4, ranks)
    a, b = scatter_step(a, me, roots, 4, ranks), scatter_step(b, me, roots, 2, ranks)
    bit = 8
    while bit < ranks:
        a, b = middle_step(a, me, roots, bit, ranks), middle_step(b, me, roots, bit, ranks)
        bit *= 2
    a, b = gather_step(a, me, 4, ranks), gather_step(b, me, 2, ranks)
    a, b = gather_step(a, me, 2, ranks), gather_step(b, me, 4, ranks)
    return gather_step(jnp.concatenate([a, b], axis=1), me, 1, ranks)


def gather_table(x, me, ranks):
    bit = 1
    while bit < ranks:
        got = swap(x, bit, ranks)
        high = (me & bit) != 0
        x = jnp.concatenate([jnp.where(high, got, x), jnp.where(high, x, got)], axis=0)
        bit *= 2
    return x


def nonzero_tiles(mask):
    ones = (mask != 0).astype(jnp.int32)
    places = jnp.arange(MT * KPT, dtype=jnp.int32)
    earlier = (places[None, :] < places[:, None]).astype(jnp.int32)
    before = jnp.sum(ones[..., None, :] * earlier, axis=-1)
    hit = ones[..., None, :] * (before[..., None, :] == jnp.arange(PCAP)[:, None])
    return jnp.sum(hit * places, axis=-1)


def ranks_of(owners, keep, direct):
    order = jnp.arange(TILES)
    earlier = order[None, :] < order[:, None]
    same = (owners[:, :, None] == owners[:, None, :]) & earlier
    rank = jnp.sum(same, axis=2, dtype=jnp.int32)
    kept_rank = jnp.sum(same & keep[:, None, :], axis=2, dtype=jnp.int32)
    spills = keep & (kept_rank >= direct)
    spill_place = jnp.sum(spills[:, None, :] & earlier, axis=2, dtype=jnp.int32)
    return rank, kept_rank, spills, spill_place


def pack_kernel(tile_ref, panel_ref, out_ref, sem):
    copies = []
    for i in range(PCAP):
        place = tile_ref[i]
        m, k = place // KPT, lax.rem(place, KPT)
        copies.append(
            pltpu.make_async_copy(
                panel_ref.at[
                    pl.ds(pl.multiple_of(m * TILE, TILE), TILE), pl.ds(pl.multiple_of(k * TILE, TILE), TILE)
                ],
                out_ref.at[pl.ds(i * TILE, TILE)],
                sem.at[i],
            )
        )
    for copy in copies:
        copy.start()
    for copy in copies:
        copy.wait()


def pack(panel, tiles):
    return pl.pallas_call(
        pack_kernel,
        out_shape=jax.ShapeDtypeStruct((PCAP * TILE, TILE), jnp.bfloat16),
        in_specs=[SMEM, ANY],
        out_specs=VMEM,
        scratch_shapes=[pltpu.SemaphoreType.DMA((PCAP,))],
        name="pack_panel",
    )(tiles, panel)


def ladder_kernel(split, tile_ref, place_ref, amp_ref, v_ref, mask_ref, out_ref, spill_ref, acc, staged, sem):
    step = pl.program_id(0)
    acc[...] = jnp.zeros_like(acc)
    for s in range(SECTIONS):
        for i in range(PCAP):
            place = tile_ref[s * PCAP + i]
            m, k = place // KPT, lax.rem(place, KPT)
            masked = v_ref[s, pl.ds(pl.multiple_of(k * TILE, TILE), TILE), :] * mask_ref[s, k]
            acc[m] += jnp.dot(
                amp_ref[s, i * TILE : (i + 1) * TILE, :], masked, preferred_element_type=jnp.float32
            )

    def copy_to(q, ref, place):
        return pltpu.make_async_copy(staged.at[q], ref.at[place], sem.at[q])

    for j in range(STEP_TILES):
        for m in range(MT):
            q = (step * STEP_TILES + j) * MT + m
            staged[q] = acc[m, :, j * TILE : (j + 1) * TILE].astype(jnp.bfloat16)
            place = place_ref[q]

            @pl.when((place >= 0) & (place < split))
            def _():
                copy_to(q, out_ref, place).start()

            @pl.when(place >= split)
            def _():
                copy_to(q, spill_ref, place - split).start()

    @pl.when(step == NT_DEV // STEP_TILES - 1)
    def _():
        def finish(q, carry):
            @pl.when(place_ref[q] >= 0)
            def _():
                copy_to(q, out_ref, 0).wait()

            return carry

        lax.fori_loop(0, TILES, finish, 0)


def ladder(amp, amp_tiles, v_blocks, v_rows, places, split):
    return pl.pallas_call(
        functools.partial(ladder_kernel, split),
        out_shape=(
            jax.ShapeDtypeStruct((split, TILE, TILE), jnp.bfloat16),
            jax.ShapeDtypeStruct((SPILL, TILE, TILE), jnp.bfloat16),
        ),
        grid=(NT_DEV // STEP_TILES,),
        in_specs=[
            SMEM,
            SMEM,
            VMEM,
            pl.BlockSpec((SECTIONS, KPT * TILE, STEP_COLS), lambda j: (0, 0, j)),
            pl.BlockSpec((SECTIONS, KPT, 1, STEP_COLS), lambda j: (0, 0, 0, j)),
        ],
        out_specs=(ANY, ANY),
        scratch_shapes=[
            pltpu.VMEM((MT, TILE, STEP_COLS), jnp.float32),
            pltpu.VMEM((TILES, TILE, TILE), jnp.bfloat16),
            pltpu.SemaphoreType.DMA((TILES,)),
        ],
        compiler_params=pltpu.CompilerParams(vmem_limit_bytes=48 * 1024 * 1024),
        name="ladder",
    )(amp_tiles, places, amp, v_blocks, v_rows)


def place_kernel(slots, split, table_ref, direct_ref, spill_ref, out_ref, zero, held, in_sem, out_sem):
    zero[...] = jnp.zeros_like(zero)

    def fetch(ref, place, j):
        return pltpu.make_async_copy(ref.at[place], held.at[j], in_sem.at[j])

    def begin(j, carry):
        source = table_ref[j]

        @pl.when((source >= 0) & (source < split))
        def _():
            fetch(direct_ref, source, j).start()

        @pl.when(source >= split)
        def _():
            fetch(spill_ref, source - split, j).start()

        @pl.when(source < 0)
        def _():
            pltpu.make_async_copy(zero, out_ref.at[j], out_sem.at[j]).start()

        return carry

    def forward(j, carry):
        @pl.when(table_ref[j] >= 0)
        def _():
            fetch(direct_ref, 0, j).wait()
            pltpu.make_async_copy(held.at[j], out_ref.at[j], out_sem.at[j]).start()

        return carry

    def finish(j, carry):
        pltpu.make_async_copy(zero, out_ref.at[j], out_sem.at[j]).wait()
        return carry

    lax.fori_loop(0, slots, begin, 0)
    lax.fori_loop(0, slots, forward, 0)
    lax.fori_loop(0, slots, finish, 0)


def place_tiles(table, direct, spill):
    slots, split = table.shape[0], direct.shape[0]
    return pl.pallas_call(
        functools.partial(place_kernel, slots, split),
        out_shape=jax.ShapeDtypeStruct((slots, TILE, TILE), jnp.bfloat16),
        in_specs=[SMEM, ANY, ANY],
        out_specs=ANY,
        scratch_shapes=[
            pltpu.VMEM((TILE, TILE), jnp.bfloat16),
            pltpu.VMEM((slots, TILE, TILE), jnp.bfloat16),
            pltpu.SemaphoreType.DMA((slots,)),
            pltpu.SemaphoreType.DMA((slots,)),
        ],
        compiler_params=pltpu.CompilerParams(vmem_limit_bytes=32 * 1024 * 1024),
        name="place_tiles",
    )(table, direct, spill)


def exchange(tiles, ranks):
    count = tiles.shape[0] // ranks
    sent = tiles.reshape(ranks, count, TILE, TILE)
    return lax.all_to_all(sent, "row", split_axis=0, concat_axis=0, tiled=True).reshape(
        ranks * count, TILE, TILE
    )


def local(t2_panels, t2_mask, v_blocks, v_mask, r_mask, owner_map, section_owner):
    ranks, groups = lax.axis_size("row"), lax.axis_size("groups")
    me = lax.axis_index("row")
    slots_each = max(2, 2 * TILES // ranks)
    direct = slots_each // 2
    roots = section_owner

    packed = pack(t2_panels[0], nonzero_tiles(t2_mask.reshape(MT * KPT)))
    amp = spread(
        jnp.broadcast_to(packed[None], (SECTIONS,) + packed.shape), me, roots, ranks
    )

    own_code = owner_map.reshape(1, TILES) * 2 + (r_mask.T.reshape(1, TILES) != 0).astype(jnp.int32)
    codes = gather_table(
        jnp.concatenate([own_code, t2_mask.reshape(1, MT * KPT)], axis=1), me, ranks
    )
    owners, keep = codes[:, :TILES] // 2, codes[:, :TILES] % 2 != 0
    amp_tiles = nonzero_tiles(jnp.take(codes[:, TILES:], roots, axis=0)).reshape(-1)
    rank, kept_rank, spills, spill_place = ranks_of(owners, keep, direct)
    most = jnp.max(jnp.sum(spills, axis=1, dtype=jnp.int32)).reshape(1, 1)
    worst = most
    for turn in range(1, groups):
        worst = jnp.maximum(
            worst, lax.ppermute(most, "groups", [(g, (g + turn) % groups) for g in range(groups)])
        )

    device = jnp.arange(ranks, dtype=jnp.int32)[:, None]
    slot = jnp.arange(slots_each, dtype=jnp.int32)
    arrives = ((owners == me) & keep)[:, None, :] & (rank[:, None, :] == slot[None, :, None])

    def row_of(x):
        return lax.dynamic_index_in_dim(x, me, 0, keepdims=False)

    def table_of(origin):
        return (jnp.sum(jnp.where(arrives, origin[:, None, :] + 1, 0), axis=2) - 1).reshape(-1)

    v_rows = jnp.repeat(v_mask.astype(jnp.bfloat16), TILE, axis=2)[:, :, None, :]

    split = ranks * direct
    short_places = row_of(
        jnp.where(keep, jnp.where(spills, split + spill_place, owners * direct + kept_rank), -1)
    )
    short_table = table_of(
        jnp.where(spills, split + device * SPILL + spill_place, device * direct + kept_rank)
    )
    long_places = row_of(jnp.where(keep, owners * slots_each + kept_rank, -1))
    long_table = table_of(device * slots_each + kept_rank)

    def short(amp, v_blocks):
        tiles, spill = ladder(amp, amp_tiles, v_blocks, v_rows, short_places, split)
        gathered = lax.all_gather(spill, "row", axis=0, tiled=True)
        return place_tiles(short_table, exchange(tiles, ranks), gathered)

    def long(amp, v_blocks):
        tiles, spill = ladder(amp, amp_tiles, v_blocks, v_rows, long_places, ranks * slots_each)
        return place_tiles(long_table, exchange(tiles, ranks), spill)

    delivered = lax.cond(worst[0, 0] <= SPILL, short, long, amp, v_blocks)
    return delivered.reshape(ranks, slots_each, TILE, TILE)


def solution(mesh):
    placed = (
        P(("groups", "row"), None, None),
        P(("groups", "row"), None, None),
        P("groups", None, "row"),
        P("groups", None, "row"),
        P("groups", "row"),
        P(("groups", "row"), None, None),
        P("groups"),
    )
    return jax.shard_map(
        local,
        mesh=mesh,
        in_specs=placed,
        out_specs=P(("groups", "row"), None, None, None),
        check_vma=False,
    )
```

```python
import functools

import jax
import jax.numpy as jnp
from jax import lax
from jax.experimental import pallas as pl
from jax.experimental.pallas import tpu as pltpu
from jax.sharding import PartitionSpec as P

TILE = 256
MT = 4
KPT = 5
NT_DEV = 8
SECTIONS = 2
PCAP = 10
TILES = MT * NT_DEV
SPILL = 3
STEP_TILES = 2
STEP_COLS = STEP_TILES * TILE
PAIRS = (SECTIONS * PCAP + MT) // 2
ANY = pl.BlockSpec(memory_space=pl.ANY)
HBM = pl.BlockSpec(memory_space=pltpu.HBM)
SMEM = pl.BlockSpec(memory_space=pltpu.SMEM)
VMEM = pl.BlockSpec(memory_space=pltpu.VMEM)


def swap(x, bit, ranks):
    return lax.ppermute(x, "row", [(i, i ^ bit) for i in range(ranks)])


def swap_with(x, note, bit, ranks):
    rows = x.shape[0] * x.shape[1]
    got = swap(jnp.concatenate([x.reshape(rows, -1), note], axis=0), bit, ranks)
    return got[:rows].reshape(x.shape), got[rows:]


def in_order(high, mine, got, axis):
    return jnp.concatenate([jnp.where(high, got, mine), jnp.where(high, mine, got)], axis=axis)


def near(me, roots, bit):
    return (((me ^ roots) & bit) == 0)[:, None, None]


def scatter_step(x, note, me, roots, bit, ranks):
    half = x.shape[1] // 2
    high = (me & bit) != 0
    low_rows, high_rows = x[:, :half], x[:, half:]
    own, give = jnp.where(high, high_rows, low_rows), jnp.where(high, low_rows, high_rows)
    if note is None:
        got = swap(give, bit, ranks)
    else:
        got, got_note = swap_with(give, note, bit, ranks)
        note = in_order(high, note, got_note, 0)
    return jnp.where(near(me, roots, bit), own, got), note


def middle_step(x, note, me, roots, bit, ranks):
    if note is None:
        got = swap(x, bit, ranks)
    else:
        got, got_note = swap_with(x, note, bit, ranks)
        note = in_order((me & bit) != 0, note, got_note, 0)
    return jnp.where(near(me, roots, bit), x, got), note


def gather_step(x, me, bit, ranks):
    return in_order((me & bit) != 0, x, swap(x, bit, ranks), 1)


def spread(own, give, me, roots, ranks):
    rows = own.shape[0]
    got = swap(give, 1, ranks)
    note = in_order((me & 1) != 0, give[rows : rows + 1], got[rows : rows + 1], 0)
    x = jnp.where(near(me, roots, 1), own[None], got[None, :rows])
    half = rows // 2
    a, b = x[:, :half], x[:, half:]
    a, note = scatter_step(a, note, me, roots, 2, ranks)
    b, _ = scatter_step(b, None, me, roots, 4, ranks)
    a, note = scatter_step(a, note, me, roots, 4, ranks)
    b, _ = scatter_step(b, None, me, roots, 2, ranks)
    bit = 8
    while bit < ranks:
        a, note = middle_step(a, note, me, roots, bit, ranks)
        b, _ = middle_step(b, None, me, roots, bit, ranks)
        bit *= 2
    a, b = gather_step(a, me, 4, ranks), gather_step(b, me, 2, ranks)
    a, b, note = lax.optimization_barrier((a, b, note))
    a, b = gather_step(a, me, 2, ranks), gather_step(b, me, 4, ranks)
    return gather_step(jnp.concatenate([a, b], axis=1), me, 1, ranks), note


def nonzero_tiles(mask):
    ones = (mask != 0).astype(jnp.int32)
    places = jnp.arange(MT * KPT, dtype=jnp.int32)
    earlier = (places[None, :] < places[:, None]).astype(jnp.int32)
    before = jnp.sum(ones[..., None, :] * earlier, axis=-1)
    hit = ones[..., None, :] * (before[..., None, :] == jnp.arange(PCAP)[:, None])
    return jnp.sum(hit * places, axis=-1)


def ranks_of(owners, keep, direct):
    order = jnp.arange(TILES)
    earlier = order[None, :] < order[:, None]
    same = (owners[:, :, None] == owners[:, None, :]) & earlier
    rank = jnp.sum(same, axis=2, dtype=jnp.int32)
    kept_rank = jnp.sum(same & keep[:, None, :], axis=2, dtype=jnp.int32)
    spills = keep & (kept_rank >= direct)
    spill_place = jnp.sum(spills[:, None, :] & earlier, axis=2, dtype=jnp.int32)
    return rank, kept_rank, spills, spill_place


def prepare_kernel(
    slots_each, direct, me_ref, mask_ref, owner_ref, keep_ref, panel_ref,
    own_ref, give_ref, short_ref, long_ref, spill_ref, kept, sem,
):
    half = PCAP // 2
    high = me_ref[0] % 2

    def tile_copy(place, ref, row, number):
        m, k = place // KPT, place % KPT
        return pltpu.make_async_copy(
            panel_ref.at[m * TILE : (m + 1) * TILE, k * TILE : (k + 1) * TILE],
            ref.at[pl.ds(pl.multiple_of(row * TILE, TILE), TILE)],
            sem.at[number],
        )

    number = jnp.int32(0)
    for place in range(MT * KPT):
        here = mask_ref[place] != 0
        upper = (number >= half).astype(jnp.int32)
        row = jnp.minimum(number - upper * half, half - 1)
        slot = jnp.minimum(number, PCAP - 1)

        @pl.when(here & (upper == high))
        def _(place=place, row=row, slot=slot):
            tile_copy(place, own_ref, row, slot).start()

        @pl.when(here & (upper != high))
        def _(place=place, row=row, slot=slot):
            tile_copy(place, give_ref, row, slot).start()

        number = number + here.astype(jnp.int32)

    column = lax.broadcasted_iota(jnp.int32, (16, TILE), 1)
    note = jnp.zeros((16, TILE), jnp.float32)
    for place in range(MT * KPT):
        note = jnp.where(column == TILES + place, mask_ref[place].astype(jnp.float32), note)
    for e in range(SPILL):
        spill_ref[e] = -1
    for o in range(kept.shape[0]):
        kept[o] = 0
    spilled_count = jnp.int32(0)
    for q in range(TILES):
        owner = owner_ref[q]
        keep = (keep_ref[q % MT * NT_DEV + q // MT] != 0).astype(jnp.int32)
        rank = kept[owner]
        kept[owner] = rank + keep
        over = keep * (rank >= direct).astype(jnp.int32)
        short_ref[q] = jnp.where(keep * (1 - over) != 0, owner * direct + rank, -1)
        long_ref[q] = jnp.where(keep != 0, owner * slots_each + rank, -1)

        @pl.when((over != 0) & (spilled_count < SPILL))
        def _(q=q, spilled_count=spilled_count):
            spill_ref[jnp.minimum(spilled_count, SPILL - 1)] = q

        spilled_count = spilled_count + over
        note = jnp.where(column == q, (owner * 2 + keep).astype(jnp.float32), note)
    note = jnp.where(column == TILES + MT * KPT, spilled_count.astype(jnp.float32), note)
    give_ref[half * TILE : half * TILE + 16, :] = note.astype(jnp.bfloat16)
    for number in range(PCAP):
        tile_copy(0, own_ref, 0, number).wait()


def prepare(panel, me, mask, owners, keep, ranks, slots_each, direct):
    rows = PCAP // 2 * TILE
    places = jax.ShapeDtypeStruct((TILES,), jnp.int32)
    return pl.pallas_call(
        functools.partial(prepare_kernel, slots_each, direct),
        out_shape=(
            jax.ShapeDtypeStruct((rows, TILE), jnp.bfloat16),
            jax.ShapeDtypeStruct((rows + 16, TILE), jnp.bfloat16),
            places,
            places,
            jax.ShapeDtypeStruct((SPILL,), jnp.int32),
        ),
        in_specs=[SMEM, SMEM, SMEM, SMEM, ANY],
        out_specs=(VMEM, VMEM, SMEM, SMEM, SMEM),
        scratch_shapes=[pltpu.SMEM((ranks,), jnp.int32), pltpu.SemaphoreType.DMA((PCAP,))],
        name="prepare",
    )(me, mask, owners, keep, panel)


def pair_up(tiles):
    m, k = (tiles // KPT).reshape(-1), (tiles % KPT).reshape(-1)
    count = SECTIONS * PCAP
    order = jnp.arange(count, dtype=jnp.int32)
    rows = jnp.arange(MT, dtype=jnp.int32)
    in_row = m[None, :] == rows[:, None]
    pairs = (jnp.sum(in_row, axis=1, dtype=jnp.int32) + 1) // 2
    first = jnp.sum(jnp.where(rows[None, :] < rows[:, None], pairs[None, :], 0), axis=1)
    nth = jnp.sum((m[None, :] == m[:, None]) & (order[None, :] < order[:, None]), axis=1, dtype=jnp.int32)
    member = 2 * jnp.sum(jnp.where(in_row, first[:, None], 0), axis=0) + nth
    hit = member[None, :] == jnp.arange(2 * PAIRS, dtype=jnp.int32)[:, None]
    panel_tile = jnp.sum(jnp.where(hit, order, 0), axis=1)
    none = SECTIONS * KPT
    v_tile = none + jnp.sum(jnp.where(hit, order // PCAP * KPT + k - none, 0), axis=1)
    pair_row = jnp.sum(first[None, 1:] <= jnp.arange(PAIRS, dtype=jnp.int32)[:, None], axis=1, dtype=jnp.int32)
    return pair_row, panel_tile, v_tile


def pair_product(pair, panel_tile_ref, v_tile_ref, amp_ref, v_ref, mask_ref):
    left, right = [], []
    for i in (2 * pair, 2 * pair + 1):
        v_tile = v_tile_ref[i]
        v_row = jnp.minimum(v_tile, SECTIONS * KPT - 1)
        left.append(amp_ref[pl.ds(pl.multiple_of(panel_tile_ref[i] * TILE, TILE), TILE), :])
        right.append(v_ref[pl.ds(pl.multiple_of(v_row * TILE, TILE), TILE), :] * mask_ref[v_tile])
    return jnp.dot(
        jnp.concatenate(left, axis=1), jnp.concatenate(right, axis=0), preferred_element_type=jnp.float32
    )


def ladder_kernel(
    row_ref, panel_tile_ref, v_tile_ref, place_ref, amp_ref, v_ref, mask_ref, out_ref, acc, staged, sem
):
    step = pl.program_id(0)
    acc[...] = jnp.zeros_like(acc)
    for pair in range(PAIRS):
        acc[row_ref[pair]] += pair_product(pair, panel_tile_ref, v_tile_ref, amp_ref, v_ref, mask_ref)

    def copy_to(q, place):
        return pltpu.make_async_copy(staged.at[q], out_ref.at[place], sem.at[q])

    for j in range(STEP_TILES):
        for m in range(MT):
            q = (step * STEP_TILES + j) * MT + m
            staged[q] = acc[m, :, j * TILE : (j + 1) * TILE].astype(jnp.bfloat16)

            @pl.when(place_ref[q] >= 0)
            def _():
                copy_to(q, place_ref[q]).start()

    @pl.when(step == NT_DEV // STEP_TILES - 1)
    def _():
        def finish(q, carry):
            @pl.when(place_ref[q] >= 0)
            def _():
                copy_to(q, 0).wait()

            return carry

        lax.fori_loop(0, TILES, finish, 0)


def ladder(amp, pairs, v, v_rows, places, slots):
    macs = 2 * PAIRS * TILE * TILE * NT_DEV * TILE
    return pl.pallas_call(
        ladder_kernel,
        out_shape=jax.ShapeDtypeStruct((slots, TILE, TILE), jnp.bfloat16),
        grid=(NT_DEV // STEP_TILES,),
        in_specs=[
            SMEM,
            SMEM,
            SMEM,
            SMEM,
            VMEM,
            pl.BlockSpec((SECTIONS * KPT * TILE, STEP_COLS), lambda j: (0, j)),
            pl.BlockSpec((SECTIONS * KPT + 1, 1, STEP_COLS), lambda j: (0, 0, j)),
        ],
        out_specs=HBM,
        scratch_shapes=[
            pltpu.VMEM((MT, TILE, STEP_COLS), jnp.float32),
            pltpu.VMEM((TILES, TILE, TILE), jnp.bfloat16),
            pltpu.SemaphoreType.DMA((TILES,)),
        ],
        compiler_params=pltpu.CompilerParams(vmem_limit_bytes=58 * 1024 * 1024),
        cost_estimate=pl.CostEstimate(flops=4 * macs, bytes_accessed=24 * 1024 * 1024, transcendentals=0),
        name="ladder",
    )(*pairs, places, amp, v, v_rows)


def spill_kernel(
    tile_ref, row_ref, panel_tile_ref, v_tile_ref, amp_ref, v_ref, mask_ref, out_ref, acc
):
    acc[...] = jnp.zeros_like(acc)
    tile = tile_ref[pl.program_id(0)]
    for pair in range(PAIRS):

        @pl.when((tile >= 0) & (row_ref[pair] == lax.rem(tile, MT)))
        def _():
            acc[...] += pair_product(pair, panel_tile_ref, v_tile_ref, amp_ref, v_ref, mask_ref)

    out_ref[0] = acc[...].astype(jnp.bfloat16)


def spilled(amp, pairs, v, v_rows, tiles):
    def column(e, tile_ref, *_):
        return jnp.maximum(tile_ref[e], 0) // MT

    return pl.pallas_call(
        spill_kernel,
        out_shape=jax.ShapeDtypeStruct((SPILL, TILE, TILE), jnp.bfloat16),
        grid_spec=pltpu.PrefetchScalarGridSpec(
            num_scalar_prefetch=4,
            grid=(SPILL,),
            in_specs=[
                VMEM,
                pl.BlockSpec((SECTIONS * KPT * TILE, TILE), lambda e, *refs: (0, column(e, *refs))),
                pl.BlockSpec((SECTIONS * KPT + 1, 1, TILE), lambda e, *refs: (0, 0, column(e, *refs))),
            ],
            out_specs=pl.BlockSpec((1, TILE, TILE), lambda e, *refs: (e, 0, 0)),
            scratch_shapes=[pltpu.VMEM((TILE, TILE), jnp.float32)],
        ),
        compiler_params=pltpu.CompilerParams(vmem_limit_bytes=32 * 1024 * 1024),
        name="spilled",
    )(tiles, *pairs, amp, v, v_rows)


def place_kernel(
    slots, split, reach, table_ref, direct_ref, near_ref, far_ref, out_ref, zero, held, in_sem, out_sem
):
    zero[...] = jnp.zeros_like(zero)

    def fetch(ref, place, j):
        return pltpu.make_async_copy(ref.at[place], held.at[j], in_sem.at[j])

    def begin(j, carry):
        source = table_ref[j]

        @pl.when((source >= 0) & (source < split))
        def _():
            fetch(direct_ref, source, j).start()

        @pl.when((source >= split) & (source < split + reach))
        def _():
            fetch(near_ref, source - split, j).start()

        @pl.when(source >= split + reach)
        def _():
            fetch(far_ref, source - split - reach, j).start()

        @pl.when(source < 0)
        def _():
            pltpu.make_async_copy(zero, out_ref.at[j], out_sem.at[j]).start()

        return carry

    def forward(j, carry):
        @pl.when(table_ref[j] >= 0)
        def _():
            fetch(direct_ref, 0, j).wait()
            pltpu.make_async_copy(held.at[j], out_ref.at[j], out_sem.at[j]).start()

        return carry

    def finish(j, carry):
        pltpu.make_async_copy(zero, out_ref.at[j], out_sem.at[j]).wait()
        return carry

    lax.fori_loop(0, slots, begin, 0)
    lax.fori_loop(0, slots, forward, 0)
    lax.fori_loop(0, slots, finish, 0)


def place_tiles(table, direct, near_spill, far_spill):
    slots, split, reach = table.shape[0], direct.shape[0], near_spill.shape[0]
    return pl.pallas_call(
        functools.partial(place_kernel, slots, split, reach),
        out_shape=jax.ShapeDtypeStruct((slots, TILE, TILE), jnp.bfloat16),
        in_specs=[SMEM, HBM, HBM, HBM],
        out_specs=HBM,
        scratch_shapes=[
            pltpu.VMEM((TILE, TILE), jnp.bfloat16),
            pltpu.VMEM((slots, TILE, TILE), jnp.bfloat16),
            pltpu.SemaphoreType.DMA((slots,)),
            pltpu.SemaphoreType.DMA((slots,)),
        ],
        compiler_params=pltpu.CompilerParams(vmem_limit_bytes=58 * 1024 * 1024),
        name="place_tiles",
    )(table, direct, near_spill, far_spill)


def exchange(tiles, ranks):
    count = tiles.shape[0] // ranks
    sent = tiles.reshape(ranks, count, TILE, TILE)
    return lax.all_to_all(sent, "row", split_axis=0, concat_axis=0, tiled=True).reshape(
        ranks * count, TILE, TILE
    )


def local(t2_panels, t2_mask, v_blocks, v_mask, r_mask, owner_map, section_owner):
    ranks, groups = lax.axis_size("row"), lax.axis_size("groups")
    me = lax.axis_index("row")
    slots_each = max(2, 2 * TILES // ranks)
    direct = slots_each // 2
    top = ranks // 2
    roots = section_owner

    own, give, short_places, long_places, spill_tiles = prepare(
        t2_panels[0],
        me.reshape(1),
        t2_mask.reshape(MT * KPT),
        owner_map.reshape(TILES),
        r_mask.reshape(TILES),
        ranks,
        slots_each,
        direct,
    )
    amp, notes = spread(own, give, me, roots, ranks)
    amp = amp.reshape(SECTIONS * PCAP * TILE, TILE)

    notes = notes[:, : TILES + MT * KPT + 1].astype(jnp.int32)
    owners, keep = notes[:, :TILES] // 2, notes[:, :TILES] % 2 != 0
    most = jnp.max(notes[:, -1:], axis=0, keepdims=True)
    worst = most
    for turn in range(1, groups):
        worst = jnp.maximum(
            worst, lax.ppermute(most, "groups", [(g, (g + turn) % groups) for g in range(groups)])
        )
    pairs = pair_up(nonzero_tiles(jnp.take(notes[:, TILES:-1], roots, axis=0)))
    rank, kept_rank, spills, spill_place = ranks_of(owners, keep, direct)

    v = v_blocks.reshape(SECTIONS * KPT * TILE, NT_DEV * TILE)
    v_rows = jnp.repeat(v_mask.reshape(SECTIONS * KPT, 1, NT_DEV).astype(jnp.bfloat16), TILE, axis=2)
    v_rows = jnp.pad(v_rows, ((0, 1), (0, 0), (0, 0)))

    device = jnp.arange(ranks, dtype=jnp.int32)[:, None]
    slot = jnp.arange(slots_each, dtype=jnp.int32)
    arrives = ((owners == me) & keep)[:, None, :] & (rank[:, None, :] == slot[None, :, None])

    def table_of(origin):
        return (jnp.sum(jnp.where(arrives, origin[:, None, :] + 1, 0), axis=2) - 1).reshape(-1)

    split = ranks * direct
    reach = ranks // 2 * SPILL
    spill_from = ((device ^ me) & top) // top * reach + (device & (top - 1)) * SPILL
    short_table = table_of(
        jnp.where(spills, split + spill_from + spill_place, device * direct + kept_rank)
    )
    long_table = table_of(device * slots_each + kept_rank)
    halves = [list(range(top)), list(range(top, ranks))]

    def short(amp, v, v_rows, spill_tiles, places, table, _, __):
        spill = spilled(amp, pairs, v, v_rows, spill_tiles)
        near_spill = lax.all_gather(spill, "row", axis=0, tiled=True, axis_index_groups=halves)
        other = swap(spill, top, ranks)
        tiles = ladder(amp, pairs, v, v_rows, places, split)
        other, tiles = lax.optimization_barrier((other, tiles))
        far_spill = lax.all_gather(other, "row", axis=0, tiled=True, axis_index_groups=halves)
        return place_tiles(table, exchange(tiles, ranks), near_spill, far_spill)

    def long(amp, v, v_rows, _, __, ___, places, table):
        tiles = ladder(amp, pairs, v, v_rows, places, ranks * slots_each)
        unused = jnp.zeros((1, TILE, TILE), jnp.bfloat16)
        return place_tiles(table, exchange(tiles, ranks), unused, unused)

    delivered = lax.cond(
        worst[0, 0] <= SPILL,
        short,
        long,
        amp,
        v,
        v_rows,
        spill_tiles,
        short_places,
        short_table,
        long_places,
        long_table,
    )
    return delivered.reshape(ranks, slots_each, TILE, TILE)


def solution(mesh):
    placed = (
        P(("groups", "row"), None, None),
        P(("groups", "row"), None, None),
        P("groups", None, "row"),
        P("groups", None, "row"),
        P("groups", "row"),
        P(("groups", "row"), None, None),
        P("groups"),
    )
    return jax.shard_map(
        local,
        mesh=mesh,
        in_specs=placed,
        out_specs=P(("groups", "row"), None, None, None),
        check_vma=False,
    )
```

```python
import functools

import jax
import jax.numpy as jnp
from jax import lax
from jax.experimental import pallas as pl
from jax.experimental.pallas import tpu as pltpu
from jax.sharding import PartitionSpec as P

TILE = 256
MT = 4
KPT = 5
NT_DEV = 8
SECTIONS = 2
PCAP = 10
TILES = MT * NT_DEV
SPILL = 3
STEP_TILES = 2
STEP_COLS = STEP_TILES * TILE
PAIRS = (SECTIONS * PCAP + MT) // 2
ANY = pl.BlockSpec(memory_space=pl.ANY)
HBM = pl.BlockSpec(memory_space=pltpu.HBM)
SMEM = pl.BlockSpec(memory_space=pltpu.SMEM)
VMEM = pl.BlockSpec(memory_space=pltpu.VMEM)


def swap(x, bit, ranks):
    return lax.ppermute(x, "row", [(i, i ^ bit) for i in range(ranks)])


def swap_with(x, note, bit, ranks):
    rows = x.shape[0] * x.shape[1]
    got = swap(jnp.concatenate([x.reshape(rows, -1), note], axis=0), bit, ranks)
    return got[:rows].reshape(x.shape), got[rows:]


def in_order(high, mine, got, axis):
    return jnp.concatenate([jnp.where(high, got, mine), jnp.where(high, mine, got)], axis=axis)


def near(me, roots, bit):
    return (((me ^ roots) & bit) == 0)[:, None, None]


def scatter_step(x, note, me, roots, bit, ranks):
    half = x.shape[1] // 2
    high = (me & bit) != 0
    low_rows, high_rows = x[:, :half], x[:, half:]
    own, give = jnp.where(high, high_rows, low_rows), jnp.where(high, low_rows, high_rows)
    if note is None:
        got = swap(give, bit, ranks)
    else:
        got, got_note = swap_with(give, note, bit, ranks)
        note = in_order(high, note, got_note, 0)
    return jnp.where(near(me, roots, bit), own, got), note


def middle_step(x, me, roots, bit, ranks):
    return jnp.where(near(me, roots, bit), x, swap(x, bit, ranks))


def gather_step(x, me, bit, ranks):
    return in_order((me & bit) != 0, x, swap(x, bit, ranks), 1)


def most_of_groups(most):
    groups = lax.axis_size("groups")
    worst = most
    for turn in range(1, groups):
        worst = jnp.maximum(
            worst, lax.ppermute(most, "groups", [(g, (g + turn) % groups) for g in range(groups)])
        )
    return worst


def spread(own, give, me, roots, ranks, digest):
    rows = own.shape[0]
    got = swap(give, 1, ranks)
    note = in_order((me & 1) != 0, give[rows : rows + 1], got[rows : rows + 1], 0)
    x = jnp.where(near(me, roots, 1), own[None], got[None, :rows])
    half = rows // 2
    a, b = x[:, :half], x[:, half:]
    a, note = scatter_step(a, note, me, roots, 2, ranks)
    b, _ = scatter_step(b, None, me, roots, 4, ranks)
    a, note = scatter_step(a, note, me, roots, 4, ranks)
    b, _ = scatter_step(b, None, me, roots, 2, ranks)
    bit = 8
    while bit < ranks:
        note = in_order((me & bit) != 0, note, swap(note, bit, ranks), 0)
        bit *= 2
    facts = digest(note)
    bit = 8
    while bit < ranks:
        a = middle_step(a, me, roots, bit, ranks)
        bit *= 2
    b, facts = lax.optimization_barrier((b, facts))
    bit = 8
    while bit < ranks:
        b = middle_step(b, me, roots, bit, ranks)
        bit *= 2
    worst = most_of_groups(facts[0])
    b, worst = lax.optimization_barrier((b, worst))
    a, b = gather_step(a, me, 4, ranks), gather_step(b, me, 2, ranks)
    a, b = gather_step(a, me, 2, ranks), gather_step(b, me, 4, ranks)
    mine = jnp.concatenate([a, b], axis=1)
    return mine, swap(mine, 1, ranks), worst, facts[1:]


def ranks_of(owners, keep, direct):
    order = jnp.arange(TILES)
    earlier = order[None, :] < order[:, None]
    same = (owners[:, :, None] == owners[:, None, :]) & earlier
    rank = jnp.sum(same, axis=2, dtype=jnp.int32)
    kept_rank = jnp.sum(same & keep[:, None, :], axis=2, dtype=jnp.int32)
    spills = keep & (kept_rank >= direct)
    spill_place = jnp.sum(spills[:, None, :] & earlier, axis=2, dtype=jnp.int32)
    return rank, kept_rank, spills, spill_place


def prepare_kernel(
    slots_each, direct, me_ref, mask_ref, owner_ref, keep_ref, panel_ref,
    own_ref, give_ref, short_ref, long_ref, spill_ref, kept, sem,
):
    half = PCAP // 2
    high = me_ref[0] % 2

    def tile_copy(place, ref, row, number):
        m, k = place // KPT, place % KPT
        return pltpu.make_async_copy(
            panel_ref.at[0, m * TILE : (m + 1) * TILE, k * TILE : (k + 1) * TILE],
            ref.at[pl.ds(pl.multiple_of(row * TILE, TILE), TILE)],
            sem.at[number],
        )

    number = jnp.int32(0)
    for place in range(MT * KPT):
        here = mask_ref[0, place // KPT, place % KPT] != 0
        upper = (number >= half).astype(jnp.int32)
        row = jnp.minimum(number - upper * half, half - 1)
        slot = jnp.minimum(number, PCAP - 1)

        @pl.when(here & (upper == high))
        def _(place=place, row=row, slot=slot):
            tile_copy(place, own_ref, row, slot).start()

        @pl.when(here & (upper != high))
        def _(place=place, row=row, slot=slot):
            tile_copy(place, give_ref, row, slot).start()

        number = number + here.astype(jnp.int32)

    column = lax.broadcasted_iota(jnp.int32, (16, TILE), 1)
    note = jnp.zeros((16, TILE), jnp.float32)
    for place in range(MT * KPT):
        note = jnp.where(column == TILES + place, mask_ref[0, place // KPT, place % KPT].astype(jnp.float32), note)
    for e in range(SPILL):
        spill_ref[e] = -1
    for o in range(kept.shape[0]):
        kept[o] = 0
    spilled_count = jnp.int32(0)
    for q in range(TILES):
        owner = owner_ref[q // MT, q % MT, 0]
        keep = (keep_ref[q % MT, q // MT] != 0).astype(jnp.int32)
        rank = kept[owner]
        kept[owner] = rank + keep
        over = keep * (rank >= direct).astype(jnp.int32)
        short_ref[q] = jnp.where(keep * (1 - over) != 0, owner * direct + rank, -1)
        long_ref[q] = jnp.where(keep != 0, owner * slots_each + rank, -1)

        @pl.when((over != 0) & (spilled_count < SPILL))
        def _(q=q, spilled_count=spilled_count):
            spill_ref[jnp.minimum(spilled_count, SPILL - 1)] = q

        spilled_count = spilled_count + over
        note = jnp.where(column == q, (owner * 2 + keep).astype(jnp.float32), note)
    note = jnp.where(column == TILES + MT * KPT, spilled_count.astype(jnp.float32), note)
    give_ref[half * TILE : half * TILE + 16, :] = note.astype(jnp.bfloat16)
    for number in range(PCAP):
        tile_copy(0, own_ref, 0, number).wait()


def prepare(panel, me, mask, owners, keep, ranks, slots_each, direct):
    rows = PCAP // 2 * TILE
    places = jax.ShapeDtypeStruct((TILES,), jnp.int32)
    return pl.pallas_call(
        functools.partial(prepare_kernel, slots_each, direct),
        out_shape=(
            jax.ShapeDtypeStruct((rows, TILE), jnp.bfloat16),
            jax.ShapeDtypeStruct((rows + 16, TILE), jnp.bfloat16),
            places,
            places,
            jax.ShapeDtypeStruct((SPILL,), jnp.int32),
        ),
        in_specs=[SMEM, SMEM, SMEM, SMEM, ANY],
        out_specs=(VMEM, VMEM, SMEM, SMEM, SMEM),
        scratch_shapes=[pltpu.SMEM((ranks,), jnp.int32), pltpu.SemaphoreType.DMA((PCAP,))],
        name="prepare",
    )(me, mask, owners, keep, panel)


def pair_kernel(me_ref, root_ref, note_ref, row_ref, panel_tile_ref, v_tile_ref, at_ref, most_ref):
    def listed(s, place):
        return (note_ref[root_ref[s], TILES + place] != 0).astype(jnp.int32)

    most = jnp.int32(0)
    for device in range(note_ref.shape[0]):
        most = jnp.maximum(most, note_ref[device, TILES + MT * KPT])
    most_ref[0, 0] = most
    for i in range(2 * PAIRS):
        panel_tile_ref[i] = 0
        v_tile_ref[i] = SECTIONS * KPT
    for pair in range(PAIRS):
        row_ref[pair] = MT - 1
    number = [jnp.int32(0)] * SECTIONS
    place_in_pairs = jnp.int32(0)
    for m in range(MT):
        for s in range(SECTIONS):
            for k in range(KPT):
                here = listed(s, m * KPT + k)
                upper = (number[s] >= PCAP // 2).astype(jnp.int32)
                away = (upper != me_ref[0] % 2).astype(jnp.int32)
                tile = 2 * (s * (PCAP // 2) + number[s] - upper * (PCAP // 2)) + away

                at_ref[(m * SECTIONS + s) * KPT + k] = jnp.where(here != 0, tile, -1)

                @pl.when(here != 0)
                def _(place_in_pairs=place_in_pairs, tile=tile, v_tile=s * KPT + k, m=m):
                    panel_tile_ref[place_in_pairs] = tile
                    v_tile_ref[place_in_pairs] = v_tile
                    row_ref[place_in_pairs // 2] = m

                place_in_pairs = place_in_pairs + here
                number[s] = number[s] + here
        place_in_pairs = (place_in_pairs + 1) // 2 * 2


def pair_up(me, roots, notes):
    members = jax.ShapeDtypeStruct((2 * PAIRS,), jnp.int32)
    *pairs, at, most = pl.pallas_call(
        pair_kernel,
        out_shape=(
            jax.ShapeDtypeStruct((PAIRS,), jnp.int32),
            members,
            members,
            jax.ShapeDtypeStruct((MT * SECTIONS * KPT,), jnp.int32),
            jax.ShapeDtypeStruct((1, 1), jnp.int32),
        ),
        in_specs=[SMEM, SMEM, SMEM],
        out_specs=(SMEM,) * 5,
        cost_estimate=pl.CostEstimate(flops=0, bytes_accessed=8 * 1024 * 1024, transcendentals=0),
        name="pair_up",
    )(me, roots, notes)
    return pairs, at, most


def panel_at(panel_tile, mine_ref, got_ref):
    rows = pl.ds(pl.multiple_of(panel_tile // 2 * TILE, TILE), TILE)
    return jnp.where(panel_tile % 2 == 0, mine_ref[rows, :], got_ref[rows, :])


def pair_product(pair, panel_tile_ref, v_tile_ref, mine_ref, got_ref, v_ref, mask_ref):
    left, right = [], []
    for i in (2 * pair, 2 * pair + 1):
        v_tile = v_tile_ref[i]
        left.append(panel_at(panel_tile_ref[i], mine_ref, got_ref))
        v_row = jnp.minimum(v_tile, SECTIONS * KPT - 1)
        right.append(v_ref[pl.ds(pl.multiple_of(v_row * TILE, TILE), TILE), :] * mask_ref[v_tile])
    return jnp.dot(
        jnp.concatenate(left, axis=1), jnp.concatenate(right, axis=0), preferred_element_type=jnp.float32
    )


def ladder_kernel(
    row_ref, panel_tile_ref, v_tile_ref, place_ref, mine_ref, got_ref, v_ref, mask_ref, out_ref, acc, staged, sem
):
    step = pl.program_id(0)
    acc[...] = jnp.zeros_like(acc)
    for pair in range(PAIRS):
        acc[row_ref[pair]] += pair_product(pair, panel_tile_ref, v_tile_ref, mine_ref, got_ref, v_ref, mask_ref)

    def copy_to(q, place):
        return pltpu.make_async_copy(staged.at[q], out_ref.at[place], sem.at[q])

    for j in range(STEP_TILES):
        for m in range(MT):
            q = (step * STEP_TILES + j) * MT + m
            staged[q] = acc[m, :, j * TILE : (j + 1) * TILE].astype(jnp.bfloat16)

            @pl.when(place_ref[q] >= 0)
            def _():
                copy_to(q, place_ref[q]).start()

    @pl.when(step == NT_DEV // STEP_TILES - 1)
    def _():
        def finish(q, carry):
            @pl.when(place_ref[q] >= 0)
            def _():
                copy_to(q, 0).wait()

            return carry

        lax.fori_loop(0, TILES, finish, 0)


def ladder(mine, got, pairs, v, v_rows, places, slots):
    macs = 2 * PAIRS * TILE * TILE * NT_DEV * TILE
    return pl.pallas_call(
        ladder_kernel,
        out_shape=jax.ShapeDtypeStruct((slots, TILE, TILE), jnp.bfloat16),
        grid=(NT_DEV // STEP_TILES,),
        in_specs=[
            SMEM,
            SMEM,
            SMEM,
            SMEM,
            VMEM,
            VMEM,
            pl.BlockSpec((SECTIONS * KPT * TILE, STEP_COLS), lambda j: (0, j)),
            pl.BlockSpec((SECTIONS * KPT + 1, 1, STEP_COLS), lambda j: (0, 0, j)),
        ],
        out_specs=HBM,
        scratch_shapes=[
            pltpu.VMEM((MT, TILE, STEP_COLS), jnp.float32),
            pltpu.VMEM((TILES, TILE, TILE), jnp.bfloat16),
            pltpu.SemaphoreType.DMA((TILES,)),
        ],
        compiler_params=pltpu.CompilerParams(vmem_limit_bytes=55 * 1024 * 1024),
        cost_estimate=pl.CostEstimate(flops=4 * macs, bytes_accessed=24 * 1024 * 1024, transcendentals=0),
        name="ladder",
    )(*pairs, places, mine, got, v, v_rows)


def column_of(tile):
    return pl.ds(pl.multiple_of(jnp.maximum(tile, 0) // MT * TILE, TILE), TILE)


def fetch_kernel(tile_ref, v_ref, out_ref, sem):
    copies = [
        pltpu.make_async_copy(v_ref.at[:, column_of(tile_ref[e])], out_ref.at[e], sem.at[e]) for e in range(SPILL)
    ]
    for copy in copies:
        copy.start()
    for copy in copies:
        copy.wait()


def fetch_columns(v, tiles):
    return pl.pallas_call(
        fetch_kernel,
        out_shape=jax.ShapeDtypeStruct((SPILL, v.shape[0], TILE), jnp.bfloat16),
        in_specs=[SMEM, HBM],
        out_specs=VMEM,
        scratch_shapes=[pltpu.SemaphoreType.DMA((SPILL,))],
        compiler_params=pltpu.CompilerParams(vmem_limit_bytes=16 * 1024 * 1024),
        cost_estimate=pl.CostEstimate(flops=0, bytes_accessed=8 * 1024 * 1024, transcendentals=0),
        name="fetch_columns",
    )(tiles, v)


def spill_kernel(tile_ref, at_ref, v_mask_ref, mine_ref, got_ref, v_ref, out_ref):
    for e in range(SPILL):
        tile = jnp.maximum(tile_ref[e], 0)
        left = []
        for i in range(SECTIONS * KPT):
            panel_tile = at_ref[lax.rem(tile, MT) * (SECTIONS * KPT) + i]
            counts = (panel_tile >= 0) & (v_mask_ref[i // KPT, i % KPT, tile // MT] != 0)
            value = panel_at(jnp.maximum(panel_tile, 0), mine_ref, got_ref)
            left.append(jnp.where(counts, value, jnp.zeros_like(value)))
        product = jnp.dot(jnp.concatenate(left, axis=1), v_ref[e], preferred_element_type=jnp.float32)
        out_ref[e] = product.astype(jnp.bfloat16)


def spilled(mine, got, at, columns, v_mask, tiles):
    return pl.pallas_call(
        spill_kernel,
        out_shape=jax.ShapeDtypeStruct((SPILL, TILE, TILE), jnp.bfloat16),
        in_specs=[SMEM] * 3 + [VMEM] * 3,
        out_specs=VMEM,
        compiler_params=pltpu.CompilerParams(vmem_limit_bytes=32 * 1024 * 1024),
        name="spilled",
    )(tiles, at, v_mask, mine, got, columns)


def clear_kernel(table_ref, out_ref, zero, sem):
    zero[...] = jnp.zeros_like(zero)

    def each(act):
        def visit(j, carry):
            @pl.when(table_ref[j] < 0)
            def _():
                act(pltpu.make_async_copy(zero, out_ref.at[j], sem.at[j]))

            return carry

        lax.fori_loop(0, out_ref.shape[0], visit, 0)

    each(lambda copy: copy.start())
    each(lambda copy: copy.wait())


def clear(table):
    slots = table.shape[0]
    return pl.pallas_call(
        clear_kernel,
        out_shape=jax.ShapeDtypeStruct((slots, TILE, TILE), jnp.bfloat16),
        in_specs=[SMEM],
        out_specs=HBM,
        scratch_shapes=[pltpu.VMEM((TILE, TILE), jnp.bfloat16), pltpu.SemaphoreType.DMA((slots,))],
        compiler_params=pltpu.CompilerParams(vmem_limit_bytes=55 * 1024 * 1024),
        cost_estimate=pl.CostEstimate(flops=0, bytes_accessed=8 * 1024 * 1024, transcendentals=0),
        name="clear",
    )(table)


def place_kernel(split, reach, table_ref, blank_ref, direct_ref, near_ref, far_ref, out_ref, held, in_sem, out_sem):
    slots = out_ref.shape[0]

    def fetch(ref, place, j):
        return pltpu.make_async_copy(ref.at[place], held.at[j], in_sem.at[j])

    def store(j):
        return pltpu.make_async_copy(held.at[j], out_ref.at[j], out_sem.at[j])

    def begin(j, carry):
        source = table_ref[j]

        @pl.when((source >= 0) & (source < split))
        def _():
            fetch(direct_ref, source, j).start()

        @pl.when((source >= split) & (source < split + reach))
        def _():
            fetch(near_ref, source - split, j).start()

        @pl.when(source >= split + reach)
        def _():
            fetch(far_ref, source - split - reach, j).start()

        return carry

    def forward(j, carry):
        @pl.when(table_ref[j] >= 0)
        def _():
            fetch(direct_ref, 0, j).wait()
            store(j).start()

        return carry

    def finish(j, carry):
        @pl.when(table_ref[j] >= 0)
        def _():
            store(j).wait()

        return carry

    lax.fori_loop(0, slots, begin, 0)
    lax.fori_loop(0, slots, forward, 0)
    lax.fori_loop(0, slots, finish, 0)


def place_tiles(table, blank, direct, near_spill, far_spill):
    slots, split, reach = table.shape[0], direct.shape[0], near_spill.shape[0]
    return pl.pallas_call(
        functools.partial(place_kernel, split, reach),
        out_shape=jax.ShapeDtypeStruct((slots, TILE, TILE), jnp.bfloat16),
        in_specs=[SMEM, HBM, HBM, HBM, HBM],
        out_specs=HBM,
        scratch_shapes=[
            pltpu.VMEM((slots, TILE, TILE), jnp.bfloat16),
            pltpu.SemaphoreType.DMA((slots,)),
            pltpu.SemaphoreType.DMA((slots,)),
        ],
        input_output_aliases={1: 0},
        compiler_params=pltpu.CompilerParams(vmem_limit_bytes=55 * 1024 * 1024),
        name="place_tiles",
    )(table, blank, direct, near_spill, far_spill)


def exchange(tiles, ranks):
    count = tiles.shape[0] // ranks
    sent = tiles.reshape(ranks, count, TILE, TILE)
    return lax.all_to_all(sent, "row", split_axis=0, concat_axis=0, tiled=True).reshape(
        ranks * count, TILE, TILE
    )


def local(t2_panels, t2_mask, v_blocks, v_mask, r_mask, owner_map, section_owner):
    ranks = lax.axis_size("row")
    me = lax.axis_index("row")
    slots_each = max(2, 2 * TILES // ranks)
    direct = slots_each // 2
    top = ranks // 2
    roots = section_owner

    own, give, short_places, long_places, spill_tiles = prepare(
        t2_panels,
        me.reshape(1),
        t2_mask,
        owner_map,
        r_mask,
        ranks,
        slots_each,
        direct,
    )
    v = v_blocks.reshape(SECTIONS * KPT * TILE, NT_DEV * TILE)
    v_rows = jnp.repeat(v_mask.reshape(SECTIONS * KPT, 1, NT_DEV).astype(jnp.bfloat16), TILE, axis=2)
    v_rows = jnp.pad(v_rows, ((0, 1), (0, 0), (0, 0)))
    columns = fetch_columns(v, spill_tiles)

    def digest(notes):
        notes = notes[:, : TILES + MT * KPT + 1].astype(jnp.int32)
        pairs, at, most = pair_up(me.reshape(1), roots, notes)
        return most, notes, pairs, at, columns

    mine, got, worst, (notes, pairs, at, columns) = spread(own, give, me, roots, ranks, digest)
    mine, got = mine.reshape(-1, TILE), got.reshape(-1, TILE)

    split = ranks * direct

    def table_of(notes, short):
        owners, keep = notes[:, :TILES] // 2, notes[:, :TILES] % 2 != 0
        rank, kept_rank, spills, spill_place = ranks_of(owners, keep, direct)
        device = jnp.arange(ranks, dtype=jnp.int32)[:, None]
        slot = jnp.arange(slots_each, dtype=jnp.int32)
        if short:
            far = ((device ^ me) & top) // top
            spill_from = split + far * (top * SPILL) + (device & (top - 1)) * SPILL + spill_place
            origin = jnp.where(spills, spill_from, device * direct + kept_rank)
        else:
            origin = device * slots_each + kept_rank
        arrives = ((owners == me) & keep)[:, None, :] & (rank[:, None, :] == slot[None, :, None])
        return (jnp.sum(jnp.where(arrives, origin[:, None, :] + 1, 0), axis=2) - 1).reshape(-1)

    halves = [list(range(top)), list(range(top, ranks))]

    def short(mine, got, v, v_rows, columns, notes, spill_tiles, places, _):
        spill = spilled(mine, got, at, columns, v_mask, spill_tiles)
        near_spill = lax.all_gather(spill, "row", axis=0, tiled=True, axis_index_groups=halves)
        other = swap(spill, top, ranks)
        tiles = ladder(mine, got, pairs, v, v_rows, places, split)
        other, tiles, notes = lax.optimization_barrier((other, tiles, notes))
        far_spill = lax.all_gather(other, "row", axis=0, tiled=True, axis_index_groups=halves)
        table = table_of(notes, True)
        blank = clear(table)
        return place_tiles(table, blank, exchange(tiles, ranks), near_spill, far_spill)

    def long(mine, got, v, v_rows, _, notes, __, ___, places):
        tiles = ladder(mine, got, pairs, v, v_rows, places, ranks * slots_each)
        unused = jnp.zeros((1, TILE, TILE), jnp.bfloat16)
        table = table_of(notes, False)
        return place_tiles(table, clear(table), exchange(tiles, ranks), unused, unused)

    delivered = lax.cond(
        worst[0, 0] <= SPILL,
        short,
        long,
        mine,
        got,
        v,
        v_rows,
        columns,
        notes,
        spill_tiles,
        short_places,
        long_places,
    )
    return delivered.reshape(ranks, slots_each, TILE, TILE)


def solution(mesh):
    placed = (
        P(("groups", "row"), None, None),
        P(("groups", "row"), None, None),
        P("groups", None, "row"),
        P("groups", None, "row"),
        P("groups", "row"),
        P(("groups", "row"), None, None),
        P("groups"),
    )
    return jax.shard_map(
        local,
        mesh=mesh,
        in_specs=placed,
        out_specs=P(("groups", "row"), None, None, None),
        check_vma=False,
    )
```

```python
import functools

import jax
import jax.numpy as jnp
from jax import lax
from jax.experimental import pallas as pl
from jax.experimental.pallas import tpu as pltpu
from jax.sharding import PartitionSpec as P

TILE = 256
MT = 4
KPT = 5
NT_DEV = 8
SECTIONS = 2
PCAP = 10
TILES = MT * NT_DEV
SPILL = 3
STEP_TILES = 2
STEP_COLS = STEP_TILES * TILE
PAIRS = (SECTIONS * PCAP + MT) // 2
ANY = pl.BlockSpec(memory_space=pl.ANY)
HBM = pl.BlockSpec(memory_space=pltpu.HBM)
SMEM = pl.BlockSpec(memory_space=pltpu.SMEM)
VMEM = pl.BlockSpec(memory_space=pltpu.VMEM)


def swap(x, bit, ranks):
    return lax.ppermute(x, "row", [(i, i ^ bit) for i in range(ranks)])


def swap_with(x, note, bit, ranks):
    rows = x.shape[0] * x.shape[1]
    got = swap(jnp.concatenate([x.reshape(rows, -1), note], axis=0), bit, ranks)
    return got[:rows].reshape(x.shape), got[rows:]


def near(me, roots, bit):
    return (((me ^ roots) & bit) == 0)[:, None, None]


def scatter_step(x, note, me, roots, bit, ranks):
    half = x.shape[1] // 2
    high = (me & bit) != 0
    low_rows, high_rows = x[:, :half], x[:, half:]
    own, give = jnp.where(high, high_rows, low_rows), jnp.where(high, low_rows, high_rows)
    if note is None:
        got = swap(give, bit, ranks)
    else:
        got, note = swap_with(give, note, bit, ranks)
    return jnp.where(near(me, roots, bit), own, got), note


def middle_step(x, me, roots, bit, ranks):
    return jnp.where(near(me, roots, bit), x, swap(x, bit, ranks))


def gather_step(x, me, bit, ranks):
    got, high = swap(x, bit, ranks), (me & bit) != 0
    return jnp.concatenate([jnp.where(high, got, x), jnp.where(high, x, got)], axis=1)


def most_of_groups(most):
    groups = lax.axis_size("groups")
    worst = most
    for turn in range(1, groups):
        worst = jnp.maximum(
            worst, lax.ppermute(most, "groups", [(g, (g + turn) % groups) for g in range(groups)])
        )
    return worst


def spread(own, give, me, roots, ranks, digest):
    rows = own.shape[0]
    got = swap(give, 1, ranks)
    note, xors = jnp.concatenate([give[rows : rows + 1], got[rows : rows + 1]], axis=0), [0, 1]
    x = jnp.where(near(me, roots, 1), own[None], got[None, :rows])
    half = rows // 2
    a, b = x[:, :half], x[:, half:]
    a, got_note = scatter_step(a, note, me, roots, 2, ranks)
    b, _ = scatter_step(b, None, me, roots, 4, ranks)
    across, across_xors, bit = note, xors, 8
    while bit < ranks:
        across = jnp.concatenate([across, swap(across, bit, ranks)], axis=0)
        across_xors = across_xors + [i ^ bit for i in across_xors]
        bit *= 2
    note, xors = jnp.concatenate([across, got_note], axis=0), across_xors + [2, 3]
    a, got_note = scatter_step(a, note, me, roots, 4, ranks)
    b, _ = scatter_step(b, None, me, roots, 2, ranks)
    note, xors = jnp.concatenate([note, got_note], axis=0), xors + [i ^ 4 for i in xors]
    missing = [i for i, other in enumerate(xors) if other >= 8]
    if missing:
        sent = jnp.concatenate([note[i : i + 1] for i in missing], axis=0)
        note = jnp.concatenate([note, swap(sent, 2, ranks)], axis=0)
        xors = xors + [xors[i] ^ 2 for i in missing]
    facts = digest(note, xors)
    worst = most_of_groups(facts[0])
    bit = 8
    while bit < ranks:
        a, b = middle_step(a, me, roots, bit, ranks), middle_step(b, me, roots, bit, ranks)
        bit *= 2
    a, b, worst, facts = lax.optimization_barrier((a, b, worst, facts))
    a, b = gather_step(a, me, 4, ranks), gather_step(b, me, 2, ranks)
    a, b = gather_step(a, me, 2, ranks), gather_step(b, me, 4, ranks)
    mine = jnp.concatenate([a, b], axis=1)
    return mine, swap(mine, 1, ranks), worst, facts[1:]


def ranks_of(owners, keep, direct):
    order = jnp.arange(TILES)
    earlier = order[None, :] < order[:, None]
    same = (owners[:, :, None] == owners[:, None, :]) & earlier
    rank = jnp.sum(same, axis=2, dtype=jnp.int32)
    kept_rank = jnp.sum(same & keep[:, None, :], axis=2, dtype=jnp.int32)
    spills = keep & (kept_rank >= direct)
    spill_place = jnp.sum(spills[:, None, :] & earlier, axis=2, dtype=jnp.int32)
    return rank, kept_rank, spills, spill_place


def prepare_kernel(
    slots_each, direct, me_ref, mask_ref, owner_ref, keep_ref, panel_ref,
    own_ref, give_ref, short_ref, long_ref, spill_ref, kept, sem,
):
    half = PCAP // 2
    high = me_ref[0] % 2

    def tile_copy(place, ref, row, number):
        m, k = place // KPT, place % KPT
        return pltpu.make_async_copy(
            panel_ref.at[0, m * TILE : (m + 1) * TILE, k * TILE : (k + 1) * TILE],
            ref.at[pl.ds(pl.multiple_of(row * TILE, TILE), TILE)],
            sem.at[number],
        )

    number = jnp.int32(0)
    for place in range(MT * KPT):
        here = mask_ref[0, place // KPT, place % KPT] != 0
        upper = (number >= half).astype(jnp.int32)
        row = jnp.minimum(number - upper * half, half - 1)
        slot = jnp.minimum(number, PCAP - 1)

        @pl.when(here & (upper == high))
        def _(place=place, row=row, slot=slot):
            tile_copy(place, own_ref, row, slot).start()

        @pl.when(here & (upper != high))
        def _(place=place, row=row, slot=slot):
            tile_copy(place, give_ref, row, slot).start()

        number = number + here.astype(jnp.int32)

    column = lax.broadcasted_iota(jnp.int32, (16, TILE), 1)
    note = jnp.zeros((16, TILE), jnp.float32)
    for place in range(MT * KPT):
        note = jnp.where(column == TILES + place, mask_ref[0, place // KPT, place % KPT].astype(jnp.float32), note)
    for e in range(SPILL):
        spill_ref[e] = -1
    for o in range(kept.shape[0]):
        kept[o] = 0
    spilled_count = jnp.int32(0)
    for q in range(TILES):
        owner = owner_ref[q % MT, q // MT]
        keep = (keep_ref[q % MT, q // MT] != 0).astype(jnp.int32)
        rank = kept[owner]
        kept[owner] = rank + keep
        over = keep * (rank >= direct).astype(jnp.int32)
        short_ref[q] = jnp.where(keep * (1 - over) != 0, owner * direct + rank, -1)
        long_ref[q] = jnp.where(keep != 0, owner * slots_each + rank, -1)

        @pl.when((over != 0) & (spilled_count < SPILL))
        def _(q=q, spilled_count=spilled_count):
            spill_ref[jnp.minimum(spilled_count, SPILL - 1)] = q

        spilled_count = spilled_count + over
        note = jnp.where(column == q, (owner * 2 + keep).astype(jnp.float32), note)
    note = jnp.where(column == TILES + MT * KPT, spilled_count.astype(jnp.float32), note)
    give_ref[half * TILE : half * TILE + 16, :] = note.astype(jnp.bfloat16)
    for number in range(PCAP):
        tile_copy(0, own_ref, 0, number).wait()


def prepare(panel, me, mask, owners, keep, ranks, slots_each, direct):
    rows = PCAP // 2 * TILE
    places = jax.ShapeDtypeStruct((TILES,), jnp.int32)
    return pl.pallas_call(
        functools.partial(prepare_kernel, slots_each, direct),
        out_shape=(
            jax.ShapeDtypeStruct((rows, TILE), jnp.bfloat16),
            jax.ShapeDtypeStruct((rows + 16, TILE), jnp.bfloat16),
            places,
            places,
            jax.ShapeDtypeStruct((SPILL,), jnp.int32),
        ),
        in_specs=[SMEM, SMEM, SMEM, SMEM, ANY],
        out_specs=(VMEM, VMEM, SMEM, SMEM, SMEM),
        scratch_shapes=[pltpu.SMEM((ranks,), jnp.int32), pltpu.SemaphoreType.DMA((PCAP,))],
        compiler_params=pltpu.CompilerParams(vmem_limit_bytes=62 * 1024 * 1024),
        name="prepare",
    )(me, mask, owners, keep, panel)


def pair_kernel(me_ref, root_row_ref, note_ref, row_ref, panel_tile_ref, v_tile_ref, at_ref, most_ref):
    def listed(s, place):
        return (note_ref[root_row_ref[s], TILES + place] != 0).astype(jnp.int32)

    most = jnp.int32(0)
    for device in range(note_ref.shape[0]):
        most = jnp.maximum(most, note_ref[device, TILES + MT * KPT])
    most_ref[0, 0] = most
    for i in range(2 * PAIRS):
        panel_tile_ref[i] = 0
        v_tile_ref[i] = SECTIONS * KPT
    for pair in range(PAIRS):
        row_ref[pair] = MT - 1
    number = [jnp.int32(0)] * SECTIONS
    place_in_pairs = jnp.int32(0)
    for m in range(MT):
        for s in range(SECTIONS):
            for k in range(KPT):
                here = listed(s, m * KPT + k)
                upper = (number[s] >= PCAP // 2).astype(jnp.int32)
                away = (upper != me_ref[0] % 2).astype(jnp.int32)
                tile = 2 * (s * (PCAP // 2) + number[s] - upper * (PCAP // 2)) + away

                at_ref[(m * SECTIONS + s) * KPT + k] = jnp.where(here != 0, tile, -1)

                @pl.when(here != 0)
                def _(place_in_pairs=place_in_pairs, tile=tile, v_tile=s * KPT + k, m=m):
                    panel_tile_ref[place_in_pairs] = tile
                    v_tile_ref[place_in_pairs] = v_tile
                    row_ref[place_in_pairs // 2] = m

                place_in_pairs = place_in_pairs + here
                number[s] = number[s] + here
        place_in_pairs = (place_in_pairs + 1) // 2 * 2


def pair_up(me, root_rows, notes):
    members = jax.ShapeDtypeStruct((2 * PAIRS,), jnp.int32)
    *pairs, at, most = pl.pallas_call(
        pair_kernel,
        out_shape=(
            jax.ShapeDtypeStruct((PAIRS,), jnp.int32),
            members,
            members,
            jax.ShapeDtypeStruct((MT * SECTIONS * KPT,), jnp.int32),
            jax.ShapeDtypeStruct((1, 1), jnp.int32),
        ),
        in_specs=[SMEM, SMEM, SMEM],
        out_specs=(SMEM,) * 5,
        compiler_params=pltpu.CompilerParams(vmem_limit_bytes=4 * 1024 * 1024),
        cost_estimate=pl.CostEstimate(flops=0, bytes_accessed=8 * 1024 * 1024, transcendentals=0),
        name="pair_up",
    )(me, root_rows, notes)
    return pairs, at, most


def panel_at(panel_tile, mine_ref, got_ref):
    rows = pl.ds(pl.multiple_of(panel_tile // 2 * TILE, TILE), TILE)
    return jnp.where(panel_tile % 2 == 0, mine_ref[rows, :], got_ref[rows, :])


def pair_product(pair, panel_tile_ref, v_tile_ref, mine_ref, got_ref, v_ref, mask_ref):
    left, right = [], []
    for i in (2 * pair, 2 * pair + 1):
        v_tile = v_tile_ref[i]
        left.append(panel_at(panel_tile_ref[i], mine_ref, got_ref))
        v_row = jnp.minimum(v_tile, SECTIONS * KPT - 1)
        right.append(v_ref[pl.ds(pl.multiple_of(v_row * TILE, TILE), TILE), :] * mask_ref[v_tile])
    return jnp.dot(
        jnp.concatenate(left, axis=1), jnp.concatenate(right, axis=0), preferred_element_type=jnp.float32
    )


def ladder_kernel(
    row_ref, panel_tile_ref, v_tile_ref, place_ref, mine_ref, got_ref, v_ref, mask_ref, out_ref, acc, staged, sem
):
    step = pl.program_id(0)
    acc[...] = jnp.zeros_like(acc)
    for pair in range(PAIRS):
        acc[row_ref[pair]] += pair_product(pair, panel_tile_ref, v_tile_ref, mine_ref, got_ref, v_ref, mask_ref)

    def copy_to(q, place):
        return pltpu.make_async_copy(staged.at[q], out_ref.at[place], sem.at[q])

    for j in range(STEP_TILES):
        for m in range(MT):
            q = (step * STEP_TILES + j) * MT + m
            staged[q] = acc[m, :, j * TILE : (j + 1) * TILE].astype(jnp.bfloat16)

            @pl.when(place_ref[q] >= 0)
            def _():
                copy_to(q, place_ref[q]).start()

    @pl.when(step == NT_DEV // STEP_TILES - 1)
    def _():
        def finish(q, carry):
            @pl.when(place_ref[q] >= 0)
            def _():
                copy_to(q, 0).wait()

            return carry

        lax.fori_loop(0, TILES, finish, 0)


def ladder(mine, got, pairs, v, v_rows, places, slots):
    macs = 2 * PAIRS * TILE * TILE * NT_DEV * TILE
    return pl.pallas_call(
        ladder_kernel,
        out_shape=jax.ShapeDtypeStruct((slots, TILE, TILE), jnp.bfloat16),
        grid=(NT_DEV // STEP_TILES,),
        in_specs=[
            SMEM,
            SMEM,
            SMEM,
            SMEM,
            VMEM,
            VMEM,
            pl.BlockSpec((SECTIONS * KPT * TILE, STEP_COLS), lambda j: (0, j)),
            pl.BlockSpec((SECTIONS * KPT + 1, 1, STEP_COLS), lambda j: (0, 0, j)),
        ],
        out_specs=HBM,
        scratch_shapes=[
            pltpu.VMEM((MT, TILE, STEP_COLS), jnp.float32),
            pltpu.VMEM((TILES, TILE, TILE), jnp.bfloat16),
            pltpu.SemaphoreType.DMA((TILES,)),
        ],
        compiler_params=pltpu.CompilerParams(vmem_limit_bytes=55 * 1024 * 1024),
        cost_estimate=pl.CostEstimate(flops=4 * macs, bytes_accessed=24 * 1024 * 1024, transcendentals=0),
        name="ladder",
    )(*pairs, places, mine, got, v, v_rows)


def column_of(tile):
    return pl.ds(pl.multiple_of(jnp.maximum(tile, 0) // MT * TILE, TILE), TILE)


def fetch_kernel(tile_ref, v_ref, out_ref, sem):
    copies = [
        pltpu.make_async_copy(v_ref.at[:, column_of(tile_ref[e])], out_ref.at[e], sem.at[e]) for e in range(SPILL)
    ]
    for copy in copies:
        copy.start()
    for copy in copies:
        copy.wait()


def fetch_columns(v, tiles):
    return pl.pallas_call(
        fetch_kernel,
        out_shape=jax.ShapeDtypeStruct((SPILL, v.shape[0], TILE), jnp.bfloat16),
        in_specs=[SMEM, HBM],
        out_specs=VMEM,
        scratch_shapes=[pltpu.SemaphoreType.DMA((SPILL,))],
        compiler_params=pltpu.CompilerParams(vmem_limit_bytes=16 * 1024 * 1024),
        cost_estimate=pl.CostEstimate(flops=0, bytes_accessed=8 * 1024 * 1024, transcendentals=0),
        name="fetch_columns",
    )(tiles, v)


def spill_kernel(tile_ref, at_ref, v_mask_ref, mine_ref, got_ref, v_ref, out_ref):
    for e in range(SPILL):
        tile = jnp.maximum(tile_ref[e], 0)
        left = []
        for i in range(SECTIONS * KPT):
            panel_tile = at_ref[lax.rem(tile, MT) * (SECTIONS * KPT) + i]
            counts = (panel_tile >= 0) & (v_mask_ref[i // KPT, i % KPT, tile // MT] != 0)
            value = panel_at(jnp.maximum(panel_tile, 0), mine_ref, got_ref)
            left.append(jnp.where(counts, value, jnp.zeros_like(value)))
        product = jnp.dot(jnp.concatenate(left, axis=1), v_ref[e], preferred_element_type=jnp.float32)
        out_ref[e] = product.astype(jnp.bfloat16)


def spilled(mine, got, at, columns, v_mask, tiles):
    return pl.pallas_call(
        spill_kernel,
        out_shape=jax.ShapeDtypeStruct((SPILL, TILE, TILE), jnp.bfloat16),
        in_specs=[SMEM] * 3 + [VMEM] * 3,
        out_specs=VMEM,
        compiler_params=pltpu.CompilerParams(vmem_limit_bytes=24 * 1024 * 1024),
        name="spilled",
    )(tiles, at, v_mask, mine, got, columns)


def begin_kernel(split, table_ref, near_ref, out_ref, zero, held, in_sem, out_sem):
    zero[...] = jnp.zeros_like(zero)
    slots, reach = out_ref.shape[0], near_ref.shape[0]

    def is_near(j):
        return (table_ref[j] >= split) & (table_ref[j] < split + reach)

    def fetch(j):
        return pltpu.make_async_copy(near_ref.at[jnp.maximum(table_ref[j] - split, 0)], held.at[j], in_sem.at[j])

    def start(j, carry):
        @pl.when(table_ref[j] < 0)
        def _():
            pltpu.make_async_copy(zero, out_ref.at[j], out_sem.at[j]).start()

        @pl.when(is_near(j))
        def _():
            fetch(j).start()

        return carry

    def forward(j, carry):
        @pl.when(is_near(j))
        def _():
            fetch(j).wait()
            pltpu.make_async_copy(held.at[j], out_ref.at[j], out_sem.at[j]).start()

        return carry

    def finish(j, carry):
        @pl.when((table_ref[j] < 0) | is_near(j))
        def _():
            pltpu.make_async_copy(zero, out_ref.at[j], out_sem.at[j]).wait()

        return carry

    lax.fori_loop(0, slots, start, 0)
    lax.fori_loop(0, slots, forward, 0)
    lax.fori_loop(0, slots, finish, 0)


def begin_output(table, split, near_spill):
    slots = table.shape[0]
    return pl.pallas_call(
        functools.partial(begin_kernel, split),
        out_shape=jax.ShapeDtypeStruct((slots, TILE, TILE), jnp.bfloat16),
        in_specs=[SMEM, HBM],
        out_specs=HBM,
        scratch_shapes=[
            pltpu.VMEM((TILE, TILE), jnp.bfloat16),
            pltpu.VMEM((slots, TILE, TILE), jnp.bfloat16),
            pltpu.SemaphoreType.DMA((slots,)),
            pltpu.SemaphoreType.DMA((slots,)),
        ],
        compiler_params=pltpu.CompilerParams(vmem_limit_bytes=55 * 1024 * 1024),
        cost_estimate=pl.CostEstimate(flops=0, bytes_accessed=8 * 1024 * 1024, transcendentals=0),
        name="begin_output",
    )(table, near_spill)


def place_kernel(split, far_from, table_ref, begun_ref, direct_ref, far_ref, out_ref, held, in_sem, out_sem):
    slots = out_ref.shape[0]

    def is_direct(j):
        return (table_ref[j] >= 0) & (table_ref[j] < split)

    def fetch(ref, place, j):
        return pltpu.make_async_copy(ref.at[place], held.at[j], in_sem.at[j])

    def store(j):
        return pltpu.make_async_copy(held.at[j], out_ref.at[j], out_sem.at[j])

    def begin(j, carry):
        source = table_ref[j]

        @pl.when(is_direct(j))
        def _():
            fetch(direct_ref, source, j).start()

        @pl.when(source >= far_from)
        def _():
            fetch(far_ref, source - far_from, j).start()

        return carry

    def forward(j, carry):
        @pl.when(is_direct(j) | (table_ref[j] >= far_from))
        def _():
            fetch(direct_ref, 0, j).wait()
            store(j).start()

        return carry

    def finish(j, carry):
        @pl.when(is_direct(j) | (table_ref[j] >= far_from))
        def _():
            store(j).wait()

        return carry

    lax.fori_loop(0, slots, begin, 0)
    lax.fori_loop(0, slots, forward, 0)
    lax.fori_loop(0, slots, finish, 0)


def place_tiles(table, begun, direct, far_from, far_spill):
    slots = table.shape[0]
    return pl.pallas_call(
        functools.partial(place_kernel, direct.shape[0], far_from),
        out_shape=jax.ShapeDtypeStruct((slots, TILE, TILE), jnp.bfloat16),
        in_specs=[SMEM, HBM, HBM, HBM],
        out_specs=HBM,
        scratch_shapes=[
            pltpu.VMEM((slots, TILE, TILE), jnp.bfloat16),
            pltpu.SemaphoreType.DMA((slots,)),
            pltpu.SemaphoreType.DMA((slots,)),
        ],
        input_output_aliases={1: 0},
        compiler_params=pltpu.CompilerParams(vmem_limit_bytes=55 * 1024 * 1024),
        name="place_tiles",
    )(table, begun, direct, far_spill)


def exchange(tiles, ranks):
    count = tiles.shape[0] // ranks
    sent = tiles.reshape(ranks, count, TILE, TILE)
    return lax.all_to_all(sent, "row", split_axis=0, concat_axis=0, tiled=True).reshape(
        ranks * count, TILE, TILE
    )


def local(t2_panels, t2_mask, v_blocks, v_mask, r_mask, owner_map, section_owner):
    ranks = lax.axis_size("row")
    me = lax.axis_index("row")
    slots_each = max(2, 2 * TILES // ranks)
    direct = slots_each // 2
    top = ranks // 2
    roots = section_owner

    own, give, short_places, long_places, spill_tiles = prepare(
        t2_panels,
        me.reshape(1),
        t2_mask,
        owner_map[:, :, 0].T,
        r_mask,
        ranks,
        slots_each,
        direct,
    )
    v = v_blocks.reshape(SECTIONS * KPT * TILE, NT_DEV * TILE)
    v_rows = jnp.repeat(v_mask.reshape(SECTIONS * KPT, 1, NT_DEV).astype(jnp.bfloat16), TILE, axis=2)
    v_rows = jnp.pad(v_rows, ((0, 1), (0, 0), (0, 0)))
    columns = fetch_columns(v, spill_tiles)

    def digest(notes, xors):
        notes = notes[:, : TILES + MT * KPT + 1].astype(jnp.int32)
        devices = me ^ jnp.asarray(xors, jnp.int32)
        order = jnp.arange(ranks, dtype=jnp.int32)
        root_rows = jnp.sum(jnp.where(devices[None, :] == roots[:, None], order, 0), axis=1)
        pairs, at, most = pair_up(me.reshape(1), root_rows, notes)
        return most, notes, devices, pairs, at, columns

    mine, got, worst, (notes, devices, pairs, at, columns) = spread(own, give, me, roots, ranks, digest)
    mine, got = mine.reshape(-1, TILE), got.reshape(-1, TILE)

    split = ranks * direct

    def table_of(notes, short):
        owners, keep = notes[:, :TILES] // 2, notes[:, :TILES] % 2 != 0
        rank, kept_rank, spills, spill_place = ranks_of(owners, keep, direct)
        device = devices[:, None]
        slot = jnp.arange(slots_each, dtype=jnp.int32)
        if short:
            far = ((device ^ me) & top) // top
            spill_from = split + far * (top * SPILL) + (device & (top - 1)) * SPILL + spill_place
            origin = jnp.where(spills, spill_from, device * direct + kept_rank)
        else:
            origin = device * slots_each + kept_rank
        arrives = ((owners == me) & keep)[:, None, :] & (rank[:, None, :] == slot[None, :, None])
        listed = jnp.sum(jnp.where(arrives, origin[:, None, :] + 1, 0), axis=2)
        in_place = devices[None, :] == jnp.arange(ranks, dtype=jnp.int32)[:, None]
        return (jnp.sum(jnp.where(in_place[:, :, None], listed[None], 0), axis=1) - 1).reshape(-1)

    halves = [list(range(top)), list(range(top, ranks))]

    def short(mine, got, v, v_rows, columns, notes, spill_tiles, places, _):
        spill = spilled(mine, got, at, columns, v_mask, spill_tiles)
        near_spill = lax.all_gather(spill, "row", axis=0, tiled=True, axis_index_groups=halves)
        other = swap(spill, top, ranks)
        tiles = ladder(mine, got, pairs, v, v_rows, places, split)
        other, tiles, notes = lax.optimization_barrier((other, tiles, notes))
        far_spill = lax.all_gather(other, "row", axis=0, tiled=True, axis_index_groups=halves)
        table = table_of(notes, True)
        begun = begin_output(table, split, near_spill)
        far_from = split + near_spill.shape[0]
        return place_tiles(table, begun, exchange(tiles, ranks), far_from, far_spill)

    def long(mine, got, v, v_rows, _, notes, __, ___, places):
        tiles = ladder(mine, got, pairs, v, v_rows, places, ranks * slots_each)
        unused = jnp.zeros((1, TILE, TILE), jnp.bfloat16)
        table = table_of(notes, False)
        begun = begin_output(table, ranks * slots_each, unused)
        return place_tiles(table, begun, exchange(tiles, ranks), ranks * slots_each + 1, unused)

    delivered = lax.cond(
        worst[0, 0] <= SPILL,
        short,
        long,
        mine,
        got,
        v,
        v_rows,
        columns,
        notes,
        spill_tiles,
        short_places,
        long_places,
    )
    return delivered.reshape(ranks, slots_each, TILE, TILE)


def solution(mesh):
    placed = (
        P(("groups", "row"), None, None),
        P(("groups", "row"), None, None),
        P("groups", None, "row"),
        P("groups", None, "row"),
        P("groups", "row"),
        P(("groups", "row"), None, None),
        P("groups"),
    )
    return jax.shard_map(
        local,
        mesh=mesh,
        in_specs=placed,
        out_specs=P(("groups", "row"), None, None, None),
        check_vma=False,
    )
```

```python
import functools

import jax
import jax.numpy as jnp
from jax import lax
from jax.experimental import pallas as pl
from jax.experimental.pallas import tpu as pltpu
from jax.sharding import PartitionSpec as P

TILE = 256
MT = 4
KPT = 5
NT_DEV = 8
SECTIONS = 2
PCAP = 10
TILES = MT * NT_DEV
SPILL = 3
SPILL_TERMS = 4
STEP_TILES = 2
STEP_COLS = STEP_TILES * TILE
PAIRS = (SECTIONS * PCAP + MT) // 2
ANY = pl.BlockSpec(memory_space=pl.ANY)
HBM = pl.BlockSpec(memory_space=pltpu.HBM)
SMEM = pl.BlockSpec(memory_space=pltpu.SMEM)
VMEM = pl.BlockSpec(memory_space=pltpu.VMEM)


def swap(x, bit, ranks):
    return lax.ppermute(x, "row", [(i, i ^ bit) for i in range(ranks)])


def swap_with(x, note, bit, ranks):
    rows = x.shape[0] * x.shape[1]
    got = swap(jnp.concatenate([x.reshape(rows, -1), note], axis=0), bit, ranks)
    return got[:rows].reshape(x.shape), got[rows:]


def near(me, roots, bit):
    return (((me ^ roots) & bit) == 0)[:, None, None]


def scatter_step(x, note, me, roots, bit, ranks):
    half = x.shape[1] // 2
    high = (me & bit) != 0
    low_rows, high_rows = x[:, :half], x[:, half:]
    own, give = jnp.where(high, high_rows, low_rows), jnp.where(high, low_rows, high_rows)
    if note is None:
        got = swap(give, bit, ranks)
    else:
        got, note = swap_with(give, note, bit, ranks)
    return jnp.where(near(me, roots, bit), own, got), note


def middle_step(x, me, roots, bit, ranks):
    return jnp.where(near(me, roots, bit), x, swap(x, bit, ranks))


def gather_step(x, me, bit, ranks):
    got, high = swap(x, bit, ranks), (me & bit) != 0
    return jnp.concatenate([jnp.where(high, got, x), jnp.where(high, x, got)], axis=1)


def most_of_groups(most):
    groups = lax.axis_size("groups")
    worst = most
    for turn in range(1, groups):
        worst = jnp.maximum(
            worst, lax.ppermute(most, "groups", [(g, (g + turn) % groups) for g in range(groups)])
        )
    return worst


def spread(own, give, me, roots, ranks, digest):
    rows = own.shape[0]
    got = swap(give, 1, ranks)
    note, xors = jnp.concatenate([give[rows : rows + 1], got[rows : rows + 1]], axis=0), [0, 1]
    x = jnp.where(near(me, roots, 1), own[None], got[None, :rows])
    half = rows // 2
    a, b = x[:, :half], x[:, half:]
    a, got_note = scatter_step(a, note, me, roots, 2, ranks)
    b, _ = scatter_step(b, None, me, roots, 4, ranks)
    across, across_xors, bit = note, xors, 8
    while bit < ranks:
        across = jnp.concatenate([across, swap(across, bit, ranks)], axis=0)
        across_xors = across_xors + [i ^ bit for i in across_xors]
        bit *= 2
    note, xors = jnp.concatenate([across, got_note], axis=0), across_xors + [2, 3]
    a, got_note = scatter_step(a, note, me, roots, 4, ranks)
    b, _ = scatter_step(b, None, me, roots, 2, ranks)
    note, xors = jnp.concatenate([note, got_note], axis=0), xors + [i ^ 4 for i in xors]
    missing = [i for i, other in enumerate(xors) if other >= 8]
    if missing:
        sent = jnp.concatenate([note[i : i + 1] for i in missing], axis=0)
        note = jnp.concatenate([note, swap(sent, 2, ranks)], axis=0)
        xors = xors + [xors[i] ^ 2 for i in missing]
    facts = digest(note, xors)
    worst = most_of_groups(facts[0])
    bit = 8
    while bit < ranks:
        a, b = middle_step(a, me, roots, bit, ranks), middle_step(b, me, roots, bit, ranks)
        bit *= 2
    a, b, worst, facts = lax.optimization_barrier((a, b, worst, facts))
    a, b = gather_step(a, me, 4, ranks), gather_step(b, me, 2, ranks)
    a, b = gather_step(a, me, 2, ranks), gather_step(b, me, 4, ranks)
    mine = jnp.concatenate([a, b], axis=1)
    return mine, swap(mine, 1, ranks), worst, facts[1:]


def ranks_of(owners, keep, far, direct):
    order = jnp.arange(TILES)
    earlier = order[None, :] < order[:, None]
    same = (owners[:, :, None] == owners[:, None, :]) & earlier
    rank = jnp.sum(same, axis=2, dtype=jnp.int32)
    kept_rank = jnp.sum(same & keep[:, None, :], axis=2, dtype=jnp.int32)
    spills = keep & (kept_rank >= direct)
    alike = (far[:, :, None] == far[:, None, :]) & earlier
    spill_place = jnp.sum(spills[:, None, :] & alike, axis=2, dtype=jnp.int32)
    return rank, kept_rank, spills, spill_place


def prepare_kernel(
    slots_each, direct, me_ref, mask_ref, owner_ref, keep_ref, panel_ref,
    own_ref, give_ref, short_ref, long_ref, spill_ref, goes_ref, kept, sem,
):
    half = PCAP // 2
    high = me_ref[0] % 2

    def tile_copy(place, ref, row, number):
        m, k = place // KPT, place % KPT
        return pltpu.make_async_copy(
            panel_ref.at[0, m * TILE : (m + 1) * TILE, k * TILE : (k + 1) * TILE],
            ref.at[pl.ds(pl.multiple_of(row * TILE, TILE), TILE)],
            sem.at[number],
        )

    number = jnp.int32(0)
    for place in range(MT * KPT):
        here = mask_ref[0, place // KPT, place % KPT] != 0
        upper = (number >= half).astype(jnp.int32)
        row = jnp.minimum(number - upper * half, half - 1)
        slot = jnp.minimum(number, PCAP - 1)

        @pl.when(here & (upper == high))
        def _(place=place, row=row, slot=slot):
            tile_copy(place, own_ref, row, slot).start()

        @pl.when(here & (upper != high))
        def _(place=place, row=row, slot=slot):
            tile_copy(place, give_ref, row, slot).start()

        number = number + here.astype(jnp.int32)

    column = lax.broadcasted_iota(jnp.int32, (16, TILE), 1)
    note = jnp.zeros((16, TILE), jnp.float32)
    for place in range(MT * KPT):
        note = jnp.where(column == TILES + place, mask_ref[0, place // KPT, place % KPT].astype(jnp.float32), note)
    for e in range(SPILL):
        spill_ref[e] = -1
        goes_ref[e] = -1
    for o in range(kept.shape[0]):
        kept[o] = 0
    near_count, far_count = jnp.int32(0), jnp.int32(0)
    top = kept.shape[0] // 2
    for q in range(TILES):
        owner = owner_ref[q % MT, q // MT]
        keep = (keep_ref[q % MT, q // MT] != 0).astype(jnp.int32)
        rank = kept[owner]
        kept[owner] = rank + keep
        over = keep * (rank >= direct).astype(jnp.int32)
        short_ref[q] = jnp.where(keep * (1 - over) != 0, owner * direct + rank, -1)
        long_ref[q] = jnp.where(keep != 0, owner * slots_each + rank, -1)

        far = (owner // top != me_ref[0] // top).astype(jnp.int32) * over
        near = over - far

        count = near_count + far_count

        @pl.when((over != 0) & (count < SPILL))
        def _(q=q, count=count, goes=jnp.where(far != 0, SPILL + far_count, near_count)):
            spill_ref[jnp.minimum(count, SPILL - 1)] = q
            goes_ref[jnp.minimum(count, SPILL - 1)] = goes

        far_count, near_count = far_count + far, near_count + near
        note = jnp.where(column == q, (owner * 2 + keep).astype(jnp.float32), note)
    note = jnp.where(column == TILES + MT * KPT, (near_count + far_count).astype(jnp.float32), note)
    note = jnp.where(column == TILES + MT * KPT + 1, far_count.astype(jnp.float32), note)
    give_ref[half * TILE : half * TILE + 16, :] = note.astype(jnp.bfloat16)
    for number in range(PCAP):
        tile_copy(0, own_ref, 0, number).wait()


def prepare(panel, me, mask, owners, keep, ranks, slots_each, direct):
    rows = PCAP // 2 * TILE
    places = jax.ShapeDtypeStruct((TILES,), jnp.int32)
    return pl.pallas_call(
        functools.partial(prepare_kernel, slots_each, direct),
        out_shape=(
            jax.ShapeDtypeStruct((rows, TILE), jnp.bfloat16),
            jax.ShapeDtypeStruct((rows + 16, TILE), jnp.bfloat16),
            places,
            places,
            jax.ShapeDtypeStruct((SPILL,), jnp.int32),
            jax.ShapeDtypeStruct((SPILL,), jnp.int32),
        ),
        in_specs=[SMEM, SMEM, SMEM, SMEM, ANY],
        out_specs=(VMEM, VMEM, SMEM, SMEM, SMEM, SMEM),
        scratch_shapes=[pltpu.SMEM((ranks,), jnp.int32), pltpu.SemaphoreType.DMA((PCAP,))],
        compiler_params=pltpu.CompilerParams(vmem_limit_bytes=62 * 1024 * 1024),
        name="prepare",
    )(me, mask, owners, keep, panel)


def pair_kernel(me_ref, root_row_ref, note_ref, row_ref, panel_tile_ref, v_tile_ref, at_ref, most_ref):
    def listed(s, place):
        return (note_ref[root_row_ref[s], TILES + place] != 0).astype(jnp.int32)

    for kind in range(2):
        most = jnp.int32(0)
        for device in range(note_ref.shape[0]):
            most = jnp.maximum(most, note_ref[device, TILES + MT * KPT + kind])
        most_ref[0, kind] = most
    for i in range(2 * PAIRS):
        panel_tile_ref[i] = 0
        v_tile_ref[i] = SECTIONS * KPT
    for pair in range(PAIRS):
        row_ref[pair] = MT - 1
    number = [jnp.int32(0)] * SECTIONS
    place_in_pairs = jnp.int32(0)
    for m in range(MT):
        for s in range(SECTIONS):
            for k in range(KPT):
                here = listed(s, m * KPT + k)
                upper = (number[s] >= PCAP // 2).astype(jnp.int32)
                away = (upper != me_ref[0] % 2).astype(jnp.int32)
                tile = 2 * (s * (PCAP // 2) + number[s] - upper * (PCAP // 2)) + away

                at_ref[(m * SECTIONS + s) * KPT + k] = jnp.where(here != 0, tile, -1)

                @pl.when(here != 0)
                def _(place_in_pairs=place_in_pairs, tile=tile, v_tile=s * KPT + k, m=m):
                    panel_tile_ref[place_in_pairs] = tile
                    v_tile_ref[place_in_pairs] = v_tile
                    row_ref[place_in_pairs // 2] = m

                place_in_pairs = place_in_pairs + here
                number[s] = number[s] + here
        place_in_pairs = (place_in_pairs + 1) // 2 * 2


def pair_up(me, root_rows, notes):
    members = jax.ShapeDtypeStruct((2 * PAIRS,), jnp.int32)
    *pairs, at, most = pl.pallas_call(
        pair_kernel,
        out_shape=(
            jax.ShapeDtypeStruct((PAIRS,), jnp.int32),
            members,
            members,
            jax.ShapeDtypeStruct((MT * SECTIONS * KPT,), jnp.int32),
            jax.ShapeDtypeStruct((1, 2), jnp.int32),
        ),
        in_specs=[SMEM, SMEM, SMEM],
        out_specs=(SMEM,) * 5,
        compiler_params=pltpu.CompilerParams(vmem_limit_bytes=4 * 1024 * 1024),
        cost_estimate=pl.CostEstimate(flops=0, bytes_accessed=8 * 1024 * 1024, transcendentals=0),
        name="pair_up",
    )(me, root_rows, notes)
    return pairs, at, most


def panel_at(panel_tile, mine_ref, got_ref):
    rows = pl.ds(pl.multiple_of(panel_tile // 2 * TILE, TILE), TILE)
    return jnp.where(panel_tile % 2 == 0, mine_ref[rows, :], got_ref[rows, :])


def pair_product(pair, panel_tile_ref, v_tile_ref, mine_ref, got_ref, v_ref, mask_ref):
    left, right = [], []
    for i in (2 * pair, 2 * pair + 1):
        v_tile = v_tile_ref[i]
        left.append(panel_at(panel_tile_ref[i], mine_ref, got_ref))
        v_row = jnp.minimum(v_tile, SECTIONS * KPT - 1)
        right.append(v_ref[pl.ds(pl.multiple_of(v_row * TILE, TILE), TILE), :] * mask_ref[v_tile])
    return jnp.dot(
        jnp.concatenate(left, axis=1), jnp.concatenate(right, axis=0), preferred_element_type=jnp.float32
    )


def ladder_kernel(
    row_ref, panel_tile_ref, v_tile_ref, place_ref, mine_ref, got_ref, v_ref, mask_ref, out_ref, acc, staged, sem
):
    step = pl.program_id(0)
    acc[...] = jnp.zeros_like(acc)
    for pair in range(PAIRS):
        acc[row_ref[pair]] += pair_product(pair, panel_tile_ref, v_tile_ref, mine_ref, got_ref, v_ref, mask_ref)

    def copy_to(q, place):
        return pltpu.make_async_copy(staged.at[q], out_ref.at[place], sem.at[q])

    for j in range(STEP_TILES):
        for m in range(MT):
            q = (step * STEP_TILES + j) * MT + m
            staged[q] = acc[m, :, j * TILE : (j + 1) * TILE].astype(jnp.bfloat16)

            @pl.when(place_ref[q] >= 0)
            def _():
                copy_to(q, place_ref[q]).start()

    @pl.when(step == NT_DEV // STEP_TILES - 1)
    def _():
        def finish(q, carry):
            @pl.when(place_ref[q] >= 0)
            def _():
                copy_to(q, 0).wait()

            return carry

        lax.fori_loop(0, TILES, finish, 0)


def ladder(mine, got, pairs, v, v_rows, places, slots):
    macs = 2 * PAIRS * TILE * TILE * NT_DEV * TILE
    return pl.pallas_call(
        ladder_kernel,
        out_shape=jax.ShapeDtypeStruct((slots, TILE, TILE), jnp.bfloat16),
        grid=(NT_DEV // STEP_TILES,),
        in_specs=[
            SMEM,
            SMEM,
            SMEM,
            SMEM,
            VMEM,
            VMEM,
            pl.BlockSpec((SECTIONS * KPT * TILE, STEP_COLS), lambda j: (0, j)),
            pl.BlockSpec((SECTIONS * KPT + 1, 1, STEP_COLS), lambda j: (0, 0, j)),
        ],
        out_specs=HBM,
        scratch_shapes=[
            pltpu.VMEM((MT, TILE, STEP_COLS), jnp.float32),
            pltpu.VMEM((TILES, TILE, TILE), jnp.bfloat16),
            pltpu.SemaphoreType.DMA((TILES,)),
        ],
        compiler_params=pltpu.CompilerParams(vmem_limit_bytes=55 * 1024 * 1024),
        cost_estimate=pl.CostEstimate(flops=4 * macs, bytes_accessed=24 * 1024 * 1024, transcendentals=0),
        name="ladder",
    )(*pairs, places, mine, got, v, v_rows)


def column_of(tile):
    return pl.ds(pl.multiple_of(jnp.maximum(tile, 0) // MT * TILE, TILE), TILE)


def fetch_kernel(tile_ref, v_ref, out_ref, sem):
    copies = [
        pltpu.make_async_copy(v_ref.at[:, column_of(tile_ref[e])], out_ref.at[e], sem.at[e]) for e in range(SPILL)
    ]
    for copy in copies:
        copy.start()
    for copy in copies:
        copy.wait()


def fetch_columns(v, tiles):
    return pl.pallas_call(
        fetch_kernel,
        out_shape=jax.ShapeDtypeStruct((SPILL, v.shape[0], TILE), jnp.bfloat16),
        in_specs=[SMEM, HBM],
        out_specs=VMEM,
        scratch_shapes=[pltpu.SemaphoreType.DMA((SPILL,))],
        compiler_params=pltpu.CompilerParams(vmem_limit_bytes=16 * 1024 * 1024),
        cost_estimate=pl.CostEstimate(flops=0, bytes_accessed=8 * 1024 * 1024, transcendentals=0),
        name="fetch_columns",
    )(tiles, v)


def spill_kernel(
    tile_ref, goes_ref, at_ref, v_mask_ref, mine_ref, got_ref, v_ref, near_ref, far_ref, acc, panel_tiles, v_tiles
):
    terms = SECTIONS * KPT
    for e in range(SPILL):

        @pl.when(tile_ref[e] >= 0)
        def _(e=e):
            tile, goes = tile_ref[e], goes_ref[e]
            count = jnp.int32(0)
            for i in range(terms):
                panel_tile = at_ref[lax.rem(tile, MT) * terms + i]
                counts = (panel_tile >= 0) & (v_mask_ref[i // KPT, i % KPT, tile // MT] != 0)

                @pl.when(counts)
                def _(i=i, count=count, panel_tile=panel_tile):
                    panel_tiles[count] = panel_tile
                    v_tiles[count] = i

                count = count + counts.astype(jnp.int32)
            acc[...] = jnp.zeros_like(acc)
            for first in range(0, terms, SPILL_TERMS):

                @pl.when(count > first)
                def _(first=first):
                    left, right = [], []
                    for j in range(first, min(first + SPILL_TERMS, terms)):
                        used = j < count
                        value = panel_at(jnp.where(used, panel_tiles[j], 0), mine_ref, got_ref)
                        left.append(jnp.where(used, value, jnp.zeros_like(value)))
                        rows = pl.ds(pl.multiple_of(jnp.where(used, v_tiles[j], 0) * TILE, TILE), TILE)
                        right.append(v_ref[e, rows, :])
                    acc[...] += jnp.dot(
                        jnp.concatenate(left, axis=1),
                        jnp.concatenate(right, axis=0),
                        preferred_element_type=jnp.float32,
                    )

            @pl.when(goes < SPILL)
            def _():
                near_ref[jnp.minimum(goes, SPILL - 1)] = acc[...].astype(jnp.bfloat16)

            @pl.when((goes >= SPILL) & (goes < SPILL + far_ref.shape[0]))
            def _():
                far_ref[jnp.clip(goes - SPILL, 0, far_ref.shape[0] - 1)] = acc[...].astype(jnp.bfloat16)


def spilled(far_each, mine, got, at, columns, v_mask, tiles, goes):
    terms = SECTIONS * KPT
    return pl.pallas_call(
        spill_kernel,
        out_shape=(
            jax.ShapeDtypeStruct((SPILL, TILE, TILE), jnp.bfloat16),
            jax.ShapeDtypeStruct((far_each, TILE, TILE), jnp.bfloat16),
        ),
        in_specs=[SMEM] * 4 + [VMEM] * 3,
        out_specs=(VMEM, VMEM),
        scratch_shapes=[
            pltpu.VMEM((TILE, TILE), jnp.float32),
            pltpu.SMEM((terms,), jnp.int32),
            pltpu.SMEM((terms,), jnp.int32),
        ],
        compiler_params=pltpu.CompilerParams(vmem_limit_bytes=24 * 1024 * 1024),
        name="spilled",
    )(tiles, goes, at, v_mask, mine, got, columns)


def begin_kernel(split, table_ref, near_ref, out_ref, zero, held, in_sem, out_sem):
    zero[...] = jnp.zeros_like(zero)
    slots, reach = out_ref.shape[0], near_ref.shape[0]

    def is_near(j):
        return (table_ref[j] >= split) & (table_ref[j] < split + reach)

    def fetch(j):
        return pltpu.make_async_copy(near_ref.at[jnp.maximum(table_ref[j] - split, 0)], held.at[j], in_sem.at[j])

    def start(j, carry):
        @pl.when(table_ref[j] < 0)
        def _():
            pltpu.make_async_copy(zero, out_ref.at[j], out_sem.at[j]).start()

        @pl.when(is_near(j))
        def _():
            fetch(j).start()

        return carry

    def forward(j, carry):
        @pl.when(is_near(j))
        def _():
            fetch(j).wait()
            pltpu.make_async_copy(held.at[j], out_ref.at[j], out_sem.at[j]).start()

        return carry

    def finish(j, carry):
        @pl.when((table_ref[j] < 0) | is_near(j))
        def _():
            pltpu.make_async_copy(zero, out_ref.at[j], out_sem.at[j]).wait()

        return carry

    lax.fori_loop(0, slots, start, 0)
    lax.fori_loop(0, slots, forward, 0)
    lax.fori_loop(0, slots, finish, 0)


def begin_output(table, split, near_spill):
    slots = table.shape[0]
    return pl.pallas_call(
        functools.partial(begin_kernel, split),
        out_shape=jax.ShapeDtypeStruct((slots, TILE, TILE), jnp.bfloat16),
        in_specs=[SMEM, HBM],
        out_specs=HBM,
        scratch_shapes=[
            pltpu.VMEM((TILE, TILE), jnp.bfloat16),
            pltpu.VMEM((slots, TILE, TILE), jnp.bfloat16),
            pltpu.SemaphoreType.DMA((slots,)),
            pltpu.SemaphoreType.DMA((slots,)),
        ],
        compiler_params=pltpu.CompilerParams(vmem_limit_bytes=55 * 1024 * 1024),
        cost_estimate=pl.CostEstimate(flops=0, bytes_accessed=8 * 1024 * 1024, transcendentals=0),
        name="begin_output",
    )(table, near_spill)


def place_kernel(split, far_from, table_ref, begun_ref, direct_ref, far_ref, out_ref, held, in_sem, out_sem):
    slots = out_ref.shape[0]

    def is_direct(j):
        return (table_ref[j] >= 0) & (table_ref[j] < split)

    def fetch(ref, place, j):
        return pltpu.make_async_copy(ref.at[place], held.at[j], in_sem.at[j])

    def store(j):
        return pltpu.make_async_copy(held.at[j], out_ref.at[j], out_sem.at[j])

    def begin(j, carry):
        source = table_ref[j]

        @pl.when(is_direct(j))
        def _():
            fetch(direct_ref, source, j).start()

        @pl.when(source >= far_from)
        def _():
            fetch(far_ref, source - far_from, j).start()

        return carry

    def forward(j, carry):
        @pl.when(is_direct(j) | (table_ref[j] >= far_from))
        def _():
            fetch(direct_ref, 0, j).wait()
            store(j).start()

        return carry

    def finish(j, carry):
        @pl.when(is_direct(j) | (table_ref[j] >= far_from))
        def _():
            store(j).wait()

        return carry

    lax.fori_loop(0, slots, begin, 0)
    lax.fori_loop(0, slots, forward, 0)
    lax.fori_loop(0, slots, finish, 0)


def place_tiles(table, begun, direct, far_from, far_spill):
    slots = table.shape[0]
    return pl.pallas_call(
        functools.partial(place_kernel, direct.shape[0], far_from),
        out_shape=jax.ShapeDtypeStruct((slots, TILE, TILE), jnp.bfloat16),
        in_specs=[SMEM, HBM, HBM, HBM],
        out_specs=HBM,
        scratch_shapes=[
            pltpu.VMEM((slots, TILE, TILE), jnp.bfloat16),
            pltpu.SemaphoreType.DMA((slots,)),
            pltpu.SemaphoreType.DMA((slots,)),
        ],
        input_output_aliases={1: 0},
        compiler_params=pltpu.CompilerParams(vmem_limit_bytes=55 * 1024 * 1024),
        name="place_tiles",
    )(table, begun, direct, far_spill)


def exchange(tiles, ranks):
    count = tiles.shape[0] // ranks
    sent = tiles.reshape(ranks, count, TILE, TILE)
    return lax.all_to_all(sent, "row", split_axis=0, concat_axis=0, tiled=True).reshape(
        ranks * count, TILE, TILE
    )


def local(t2_panels, t2_mask, v_blocks, v_mask, r_mask, owner_map, section_owner):
    ranks = lax.axis_size("row")
    me = lax.axis_index("row")
    slots_each = max(2, 2 * TILES // ranks)
    direct = slots_each // 2
    top = ranks // 2
    roots = section_owner

    own, give, short_places, long_places, spill_tiles, spill_goes = prepare(
        t2_panels,
        me.reshape(1),
        t2_mask,
        owner_map[:, :, 0].T,
        r_mask,
        ranks,
        slots_each,
        direct,
    )
    v = v_blocks.reshape(SECTIONS * KPT * TILE, NT_DEV * TILE)
    v_rows = jnp.repeat(v_mask.reshape(SECTIONS * KPT, 1, NT_DEV).astype(jnp.bfloat16), TILE, axis=2)
    v_rows = jnp.pad(v_rows, ((0, 1), (0, 0), (0, 0)))
    columns = fetch_columns(v, spill_tiles)

    def digest(notes, xors):
        notes = notes[:, : TILES + MT * KPT + 2].astype(jnp.int32)
        devices = me ^ jnp.asarray(xors, jnp.int32)
        order = jnp.arange(ranks, dtype=jnp.int32)
        root_rows = jnp.sum(jnp.where(devices[None, :] == roots[:, None], order, 0), axis=1)
        pairs, at, most = pair_up(me.reshape(1), root_rows, notes)
        return most, notes, devices, pairs, at, columns

    mine, got, worst, facts = spread(own, give, me, roots, ranks, digest)
    notes, devices, pairs, at, columns = facts
    mine, got = mine.reshape(-1, TILE), got.reshape(-1, TILE)

    split = ranks * direct

    def table_of(notes, far_each):
        owners, keep = notes[:, :TILES] // 2, notes[:, :TILES] % 2 != 0
        device = devices[:, None]
        rank, kept_rank, spills, spill_place = ranks_of(owners, keep, ((owners ^ device) & top) != 0, direct)
        slot = jnp.arange(slots_each, dtype=jnp.int32)
        if far_each:
            member = device & (top - 1)
            from_near = split + member * SPILL + spill_place
            from_far = split + (top * SPILL) + member * far_each + spill_place
            spilled_from = jnp.where(((device ^ me) & top) != 0, from_far, from_near)
            origin = jnp.where(spills, spilled_from, device * direct + kept_rank)
        else:
            origin = device * slots_each + kept_rank
        arrives = ((owners == me) & keep)[:, None, :] & (rank[:, None, :] == slot[None, :, None])
        listed = jnp.sum(jnp.where(arrives, origin[:, None, :] + 1, 0), axis=2)
        in_place = devices[None, :] == jnp.arange(ranks, dtype=jnp.int32)[:, None]
        return (jnp.sum(jnp.where(in_place[:, :, None], listed[None], 0), axis=1) - 1).reshape(-1)

    halves = [list(range(top)), list(range(top, ranks))]

    def gathered(spill):
        return lax.all_gather(spill, "row", axis=0, tiled=True, axis_index_groups=halves)

    def short(far_each, mine, got, v, v_rows, columns, notes, spill_tiles, spill_goes, places, _):
        near, far = spilled(far_each, mine, got, at, columns, v_mask, spill_tiles, spill_goes)
        near_spill = gathered(near)
        far = swap(far, top, ranks)
        tiles = ladder(mine, got, pairs, v, v_rows, places, split)
        far, tiles, notes = lax.optimization_barrier((far, tiles, notes))
        far_spill = gathered(far)
        table = table_of(notes, far_each)
        begun = begin_output(table, split, near_spill)
        return place_tiles(table, begun, exchange(tiles, ranks), split + top * SPILL, far_spill)

    def long(mine, got, v, v_rows, _, notes, __, ___, ____, places):
        tiles = ladder(mine, got, pairs, v, v_rows, places, ranks * slots_each)
        unused = jnp.zeros((1, TILE, TILE), jnp.bfloat16)
        table = table_of(notes, 0)
        begun = begin_output(table, ranks * slots_each, unused)
        return place_tiles(table, begun, exchange(tiles, ranks), ranks * slots_each + 1, unused)

    way = jnp.where(worst[0, 0] > SPILL, 2, (worst[0, 1] == SPILL).astype(jnp.int32))
    delivered = lax.switch(
        way,
        [functools.partial(short, SPILL - 1), functools.partial(short, SPILL), long],
        mine,
        got,
        v,
        v_rows,
        columns,
        notes,
        spill_tiles,
        spill_goes,
        short_places,
        long_places,
    )
    return delivered.reshape(ranks, slots_each, TILE, TILE)


def solution(mesh):
    placed = (
        P(("groups", "row"), None, None),
        P(("groups", "row"), None, None),
        P("groups", None, "row"),
        P("groups", None, "row"),
        P("groups", "row"),
        P(("groups", "row"), None, None),
        P("groups"),
    )
    return jax.shard_map(
        local,
        mesh=mesh,
        in_specs=placed,
        out_specs=P(("groups", "row"), None, None, None),
        check_vma=False,
    )
```

```python
import functools

import jax
import jax.numpy as jnp
from jax import lax
from jax.experimental import pallas as pl
from jax.experimental.pallas import tpu as pltpu
from jax.sharding import PartitionSpec as P

TILE = 256
MT = 4
KPT = 5
NT_DEV = 8
SECTIONS = 2
PCAP = 10
TILES = MT * NT_DEV
SPILL = 3
SPILL_TERMS = 4
STEP_TILES = 2
STEP_COLS = STEP_TILES * TILE
PAIRS = (SECTIONS * PCAP + MT) // 2
ANY = pl.BlockSpec(memory_space=pl.ANY)
HBM = pl.BlockSpec(memory_space=pltpu.HBM)
SMEM = pl.BlockSpec(memory_space=pltpu.SMEM)
VMEM = pl.BlockSpec(memory_space=pltpu.VMEM)


def swap(x, bit, ranks):
    return lax.ppermute(x, "row", [(i, i ^ bit) for i in range(ranks)])


def swap_with(x, note, bit, ranks):
    rows = x.shape[0] * x.shape[1]
    got = swap(jnp.concatenate([x.reshape(rows, -1), note], axis=0), bit, ranks)
    return got[:rows].reshape(x.shape), got[rows:]


def near(me, roots, bit):
    return (((me ^ roots) & bit) == 0)[:, None, None]


def scatter_step(x, note, me, roots, bit, ranks):
    half = x.shape[1] // 2
    high = (me & bit) != 0
    low_rows, high_rows = x[:, :half], x[:, half:]
    own, give = jnp.where(high, high_rows, low_rows), jnp.where(high, low_rows, high_rows)
    if note is None:
        got = swap(give, bit, ranks)
    else:
        got, note = swap_with(give, note, bit, ranks)
    return jnp.where(near(me, roots, bit), own, got), note


def middle_step(x, me, roots, bit, ranks):
    return jnp.where(near(me, roots, bit), x, swap(x, bit, ranks))


def gather_step(x, me, bit, ranks):
    got, high = swap(x, bit, ranks), (me & bit) != 0
    return jnp.concatenate([jnp.where(high, got, x), jnp.where(high, x, got)], axis=1)


def most_of_groups(most):
    groups = lax.axis_size("groups")
    worst = most
    for turn in range(1, groups):
        worst = jnp.maximum(
            worst, lax.ppermute(most, "groups", [(g, (g + turn) % groups) for g in range(groups)])
        )
    return worst


def spread(own, give, me, roots, ranks, digest):
    rows = own.shape[0]
    got = swap(give, 1, ranks)
    note, xors = jnp.concatenate([give[rows : rows + 1], got[rows : rows + 1]], axis=0), [0, 1]
    x = jnp.where(near(me, roots, 1), own[None], got[None, :rows])
    half = rows // 2
    a, b = x[:, :half], x[:, half:]
    a, got_note = scatter_step(a, note, me, roots, 2, ranks)
    b, _ = scatter_step(b, None, me, roots, 4, ranks)
    across, across_xors, bit = note, xors, 8
    while bit < ranks:
        across = jnp.concatenate([across, swap(across, bit, ranks)], axis=0)
        across_xors = across_xors + [i ^ bit for i in across_xors]
        bit *= 2
    note, xors = jnp.concatenate([across, got_note], axis=0), across_xors + [2, 3]
    a, got_note = scatter_step(a, note, me, roots, 4, ranks)
    b, _ = scatter_step(b, None, me, roots, 2, ranks)
    note, xors = jnp.concatenate([note, got_note], axis=0), xors + [i ^ 4 for i in xors]
    missing = [i for i, other in enumerate(xors) if other >= 8]
    if missing:
        sent = jnp.concatenate([note[i : i + 1] for i in missing], axis=0)
        note = jnp.concatenate([note, swap(sent, 2, ranks)], axis=0)
        xors = xors + [xors[i] ^ 2 for i in missing]
    facts = digest(note, xors)
    worst = most_of_groups(facts[0])
    bit = 8
    while bit < ranks:
        a, b = middle_step(a, me, roots, bit, ranks), middle_step(b, me, roots, bit, ranks)
        bit *= 2
    a, b, worst, facts = lax.optimization_barrier((a, b, worst, facts))
    a, b = gather_step(a, me, 4, ranks), gather_step(b, me, 2, ranks)
    a, b = gather_step(a, me, 2, ranks), gather_step(b, me, 4, ranks)
    mine = jnp.concatenate([a, b], axis=1)
    return mine, swap(mine, 1, ranks), worst, facts[1:]


def ranks_of(owners, keep, far, direct):
    order = jnp.arange(TILES)
    earlier = order[None, :] < order[:, None]
    same = (owners[:, :, None] == owners[:, None, :]) & earlier
    rank = jnp.sum(same, axis=2, dtype=jnp.int32)
    kept_rank = jnp.sum(same & keep[:, None, :], axis=2, dtype=jnp.int32)
    spills = keep & (kept_rank >= direct)
    alike = (far[:, :, None] == far[:, None, :]) & earlier
    spill_place = jnp.sum(spills[:, None, :] & alike, axis=2, dtype=jnp.int32)
    return rank, kept_rank, spills, spill_place


def prepare_kernel(
    slots_each, direct, me_ref, mask_ref, owner_ref, keep_ref, panel_ref,
    own_ref, give_ref, short_ref, long_ref, spill_ref, goes_ref, kept, sem,
):
    half = PCAP // 2
    high = me_ref[0] % 2

    def tile_copy(place, ref, row, number):
        m, k = place // KPT, place % KPT
        return pltpu.make_async_copy(
            panel_ref.at[0, m * TILE : (m + 1) * TILE, k * TILE : (k + 1) * TILE],
            ref.at[pl.ds(pl.multiple_of(row * TILE, TILE), TILE)],
            sem.at[number],
        )

    number = jnp.int32(0)
    for place in range(MT * KPT):
        here = mask_ref[0, place // KPT, place % KPT] != 0
        upper = (number >= half).astype(jnp.int32)
        row = jnp.minimum(number - upper * half, half - 1)
        slot = jnp.minimum(number, PCAP - 1)

        @pl.when(here & (upper == high))
        def _(place=place, row=row, slot=slot):
            tile_copy(place, own_ref, row, slot).start()

        @pl.when(here & (upper != high))
        def _(place=place, row=row, slot=slot):
            tile_copy(place, give_ref, row, slot).start()

        number = number + here.astype(jnp.int32)

    column = lax.broadcasted_iota(jnp.int32, (16, TILE), 1)
    note = jnp.zeros((16, TILE), jnp.float32)
    for place in range(MT * KPT):
        note = jnp.where(column == TILES + place, mask_ref[0, place // KPT, place % KPT].astype(jnp.float32), note)
    for e in range(SPILL):
        spill_ref[e] = -1
        goes_ref[e] = -1
    for o in range(kept.shape[0]):
        kept[o] = 0
    near_count, far_count = jnp.int32(0), jnp.int32(0)
    top = kept.shape[0] // 2
    for q in range(TILES):
        owner = owner_ref[q % MT, q // MT]
        keep = (keep_ref[q % MT, q // MT] != 0).astype(jnp.int32)
        rank = kept[owner]
        kept[owner] = rank + keep
        over = keep * (rank >= direct).astype(jnp.int32)
        short_ref[q] = jnp.where(keep * (1 - over) != 0, owner * direct + rank, -1)
        long_ref[q] = jnp.where(keep != 0, owner * slots_each + rank, -1)

        far = (owner // top != me_ref[0] // top).astype(jnp.int32) * over
        near = over - far

        count = near_count + far_count

        @pl.when((over != 0) & (count < SPILL))
        def _(q=q, count=count, goes=jnp.where(far != 0, SPILL + far_count, near_count)):
            spill_ref[jnp.minimum(count, SPILL - 1)] = q
            goes_ref[jnp.minimum(count, SPILL - 1)] = goes

        far_count, near_count = far_count + far, near_count + near
        note = jnp.where(column == q, (owner * 2 + keep).astype(jnp.float32), note)
    note = jnp.where(column == TILES + MT * KPT, (near_count + far_count).astype(jnp.float32), note)
    note = jnp.where(column == TILES + MT * KPT + 1, far_count.astype(jnp.float32), note)
    give_ref[half * TILE : half * TILE + 16, :] = note.astype(jnp.bfloat16)
    for number in range(PCAP):
        tile_copy(0, own_ref, 0, number).wait()


def prepare(panel, me, mask, owners, keep, ranks, slots_each, direct):
    rows = PCAP // 2 * TILE
    places = jax.ShapeDtypeStruct((TILES,), jnp.int32)
    return pl.pallas_call(
        functools.partial(prepare_kernel, slots_each, direct),
        out_shape=(
            jax.ShapeDtypeStruct((rows, TILE), jnp.bfloat16),
            jax.ShapeDtypeStruct((rows + 16, TILE), jnp.bfloat16),
            places,
            places,
            jax.ShapeDtypeStruct((SPILL,), jnp.int32),
            jax.ShapeDtypeStruct((SPILL,), jnp.int32),
        ),
        in_specs=[SMEM, SMEM, SMEM, SMEM, ANY],
        out_specs=(VMEM, VMEM, SMEM, SMEM, SMEM, SMEM),
        scratch_shapes=[pltpu.SMEM((ranks,), jnp.int32), pltpu.SemaphoreType.DMA((PCAP,))],
        compiler_params=pltpu.CompilerParams(vmem_limit_bytes=62 * 1024 * 1024),
        name="prepare",
    )(me, mask, owners, keep, panel)


def pair_kernel(me_ref, root_row_ref, note_ref, row_ref, panel_tile_ref, v_tile_ref, at_ref, most_ref):
    def listed(s, place):
        return (note_ref[root_row_ref[s], TILES + place] != 0).astype(jnp.int32)

    for kind in range(2):
        most = jnp.int32(0)
        for device in range(note_ref.shape[0]):
            most = jnp.maximum(most, note_ref[device, TILES + MT * KPT + kind])
        most_ref[0, kind] = most
    for i in range(2 * PAIRS):
        panel_tile_ref[i] = 0
        v_tile_ref[i] = SECTIONS * KPT
    for pair in range(PAIRS):
        row_ref[pair] = MT - 1
    number = [jnp.int32(0)] * SECTIONS
    place_in_pairs = jnp.int32(0)
    for m in range(MT):
        for s in range(SECTIONS):
            for k in range(KPT):
                here = listed(s, m * KPT + k)
                upper = (number[s] >= PCAP // 2).astype(jnp.int32)
                away = (upper != me_ref[0] % 2).astype(jnp.int32)
                tile = 2 * (s * (PCAP // 2) + number[s] - upper * (PCAP // 2)) + away

                at_ref[(m * SECTIONS + s) * KPT + k] = jnp.where(here != 0, tile, -1)

                @pl.when(here != 0)
                def _(place_in_pairs=place_in_pairs, tile=tile, v_tile=s * KPT + k, m=m):
                    panel_tile_ref[place_in_pairs] = tile
                    v_tile_ref[place_in_pairs] = v_tile
                    row_ref[place_in_pairs // 2] = m

                place_in_pairs = place_in_pairs + here
                number[s] = number[s] + here
        place_in_pairs = (place_in_pairs + 1) // 2 * 2


def pair_up(me, root_rows, notes):
    members = jax.ShapeDtypeStruct((2 * PAIRS,), jnp.int32)
    *pairs, at, most = pl.pallas_call(
        pair_kernel,
        out_shape=(
            jax.ShapeDtypeStruct((PAIRS,), jnp.int32),
            members,
            members,
            jax.ShapeDtypeStruct((MT * SECTIONS * KPT,), jnp.int32),
            jax.ShapeDtypeStruct((1, 2), jnp.int32),
        ),
        in_specs=[SMEM, SMEM, SMEM],
        out_specs=(SMEM,) * 5,
        compiler_params=pltpu.CompilerParams(vmem_limit_bytes=4 * 1024 * 1024),
        cost_estimate=pl.CostEstimate(flops=0, bytes_accessed=8 * 1024 * 1024, transcendentals=0),
        name="pair_up",
    )(me, root_rows, notes)
    return pairs, at, most


def panel_at(panel_tile, mine_ref, got_ref):
    rows = pl.ds(pl.multiple_of(panel_tile // 2 * TILE, TILE), TILE)
    return jnp.where(panel_tile % 2 == 0, mine_ref[rows, :], got_ref[rows, :])


def pair_product(pair, panel_tile_ref, v_tile_ref, mine_ref, got_ref, v_ref, v_mask_ref, first_column):
    left, right = [], []
    tile_of = lax.broadcasted_iota(jnp.int32, (1, STEP_COLS), 1) // TILE
    for i in (2 * pair, 2 * pair + 1):
        v_tile = v_tile_ref[i]
        left.append(panel_at(panel_tile_ref[i], mine_ref, got_ref))
        v_row = jnp.minimum(v_tile, SECTIONS * KPT - 1)
        mask = jnp.zeros((1, STEP_COLS), jnp.float32)
        for j in range(STEP_TILES):
            kept = (v_mask_ref[v_row // KPT, lax.rem(v_row, KPT), first_column + j] != 0) & (v_row == v_tile)
            mask = jnp.where(tile_of == j, kept.astype(jnp.float32), mask)
        right.append(v_ref[pl.ds(pl.multiple_of(v_row * TILE, TILE), TILE), :] * mask.astype(jnp.bfloat16))
    return jnp.dot(
        jnp.concatenate(left, axis=1), jnp.concatenate(right, axis=0), preferred_element_type=jnp.float32
    )


def ladder_kernel(
    row_ref, panel_tile_ref, v_tile_ref, place_ref, v_mask_ref, mine_ref, got_ref, v_ref, out_ref, acc, staged, sem
):
    step = pl.program_id(0)
    acc[...] = jnp.zeros_like(acc)
    for pair in range(PAIRS):
        acc[row_ref[pair]] += pair_product(
            pair, panel_tile_ref, v_tile_ref, mine_ref, got_ref, v_ref, v_mask_ref, step * STEP_TILES
        )

    def copy_to(q, place):
        return pltpu.make_async_copy(staged.at[q], out_ref.at[place], sem.at[q])

    for j in range(STEP_TILES):
        for m in range(MT):
            q = (step * STEP_TILES + j) * MT + m
            staged[q] = acc[m, :, j * TILE : (j + 1) * TILE].astype(jnp.bfloat16)

            @pl.when(place_ref[q] >= 0)
            def _():
                copy_to(q, place_ref[q]).start()

    @pl.when(step == NT_DEV // STEP_TILES - 1)
    def _():
        def finish(q, carry):
            @pl.when(place_ref[q] >= 0)
            def _():
                copy_to(q, 0).wait()

            return carry

        lax.fori_loop(0, TILES, finish, 0)


def ladder(mine, got, pairs, v, v_mask, places, slots):
    macs = 2 * PAIRS * TILE * TILE * NT_DEV * TILE
    return pl.pallas_call(
        ladder_kernel,
        out_shape=jax.ShapeDtypeStruct((slots, TILE, TILE), jnp.bfloat16),
        grid=(NT_DEV // STEP_TILES,),
        in_specs=[
            SMEM,
            SMEM,
            SMEM,
            SMEM,
            SMEM,
            VMEM,
            VMEM,
            pl.BlockSpec((SECTIONS * KPT * TILE, STEP_COLS), lambda j: (0, j)),
        ],
        out_specs=HBM,
        scratch_shapes=[
            pltpu.VMEM((MT, TILE, STEP_COLS), jnp.float32),
            pltpu.VMEM((TILES, TILE, TILE), jnp.bfloat16),
            pltpu.SemaphoreType.DMA((TILES,)),
        ],
        compiler_params=pltpu.CompilerParams(vmem_limit_bytes=55 * 1024 * 1024),
        cost_estimate=pl.CostEstimate(flops=4 * macs, bytes_accessed=24 * 1024 * 1024, transcendentals=0),
        name="ladder",
    )(*pairs, places, v_mask, mine, got, v)


def column_of(tile):
    return pl.ds(pl.multiple_of(jnp.maximum(tile, 0) // MT * TILE, TILE), TILE)


def fetch_kernel(tile_ref, v_ref, out_ref, sem):
    copies = [
        pltpu.make_async_copy(v_ref.at[:, column_of(tile_ref[e])], out_ref.at[e], sem.at[e]) for e in range(SPILL)
    ]
    for copy in copies:
        copy.start()
    for copy in copies:
        copy.wait()


def fetch_columns(v, tiles):
    return pl.pallas_call(
        fetch_kernel,
        out_shape=jax.ShapeDtypeStruct((SPILL, v.shape[0], TILE), jnp.bfloat16),
        in_specs=[SMEM, HBM],
        out_specs=VMEM,
        scratch_shapes=[pltpu.SemaphoreType.DMA((SPILL,))],
        compiler_params=pltpu.CompilerParams(vmem_limit_bytes=16 * 1024 * 1024),
        cost_estimate=pl.CostEstimate(flops=0, bytes_accessed=8 * 1024 * 1024, transcendentals=0),
        name="fetch_columns",
    )(tiles, v)


def spill_kernel(
    tile_ref, goes_ref, at_ref, v_mask_ref, mine_ref, got_ref, v_ref, near_ref, far_ref, acc, panel_tiles, v_tiles
):
    terms = SECTIONS * KPT
    counts = []
    for e in range(SPILL):
        tile = jnp.maximum(tile_ref[e], 0)
        count = jnp.int32(0)
        for i in range(terms):
            panel_tile = at_ref[lax.rem(tile, MT) * terms + i]
            panel_tiles[e * (terms + 1) + count] = panel_tile
            v_tiles[e * (terms + 1) + count] = i
            counted = (panel_tile >= 0) & (v_mask_ref[i // KPT, i % KPT, tile // MT] != 0)
            count = count + counted.astype(jnp.int32)
        counts.append(count)

    def product(e, first):
        left, right = [], []
        for j in range(first, min(first + SPILL_TERMS, terms)):
            used = j < counts[e]
            value = panel_at(jnp.where(used, panel_tiles[e * (terms + 1) + j], 0), mine_ref, got_ref)
            left.append(jnp.where(used, value, jnp.zeros_like(value)))
            v_row = jnp.where(used, v_tiles[e * (terms + 1) + j], 0)
            right.append(v_ref[e, pl.ds(pl.multiple_of(v_row * TILE, TILE), TILE), :])
        return jnp.dot(
            jnp.concatenate(left, axis=1), jnp.concatenate(right, axis=0), preferred_element_type=jnp.float32
        )

    for e in range(SPILL):
        acc[e] = product(e, 0)
    for e in range(SPILL):
        for first in range(SPILL_TERMS, terms, SPILL_TERMS):

            @pl.when((counts[e] > first) & (tile_ref[e] >= 0))
            def _(e=e, first=first):
                acc[e] += product(e, first)

        goes = goes_ref[e]

        @pl.when((goes >= 0) & (goes < SPILL))
        def _(e=e, goes=goes):
            near_ref[jnp.clip(goes, 0, SPILL - 1)] = acc[e].astype(jnp.bfloat16)

        @pl.when((goes >= SPILL) & (goes < SPILL + far_ref.shape[0]))
        def _(e=e, goes=goes):
            far_ref[jnp.clip(goes - SPILL, 0, far_ref.shape[0] - 1)] = acc[e].astype(jnp.bfloat16)


def spilled(far_each, mine, got, at, columns, v_mask, tiles, goes):
    terms = SECTIONS * KPT
    return pl.pallas_call(
        spill_kernel,
        out_shape=(
            jax.ShapeDtypeStruct((SPILL, TILE, TILE), jnp.bfloat16),
            jax.ShapeDtypeStruct((far_each, TILE, TILE), jnp.bfloat16),
        ),
        in_specs=[SMEM] * 4 + [VMEM] * 3,
        out_specs=(VMEM, VMEM),
        scratch_shapes=[
            pltpu.VMEM((SPILL, TILE, TILE), jnp.float32),
            pltpu.SMEM((SPILL * (terms + 1),), jnp.int32),
            pltpu.SMEM((SPILL * (terms + 1),), jnp.int32),
        ],
        compiler_params=pltpu.CompilerParams(vmem_limit_bytes=24 * 1024 * 1024),
        name="spilled",
    )(tiles, goes, at, v_mask, mine, got, columns)


def begin_kernel(split, table_ref, near_ref, out_ref, zero, held, in_sem, out_sem):
    zero[...] = jnp.zeros_like(zero)
    slots, reach = out_ref.shape[0], near_ref.shape[0]

    def is_near(j):
        return (table_ref[j] >= split) & (table_ref[j] < split + reach)

    def fetch(j):
        return pltpu.make_async_copy(near_ref.at[jnp.maximum(table_ref[j] - split, 0)], held.at[j], in_sem.at[j])

    def start(j, carry):
        @pl.when(table_ref[j] < 0)
        def _():
            pltpu.make_async_copy(zero, out_ref.at[j], out_sem.at[j]).start()

        @pl.when(is_near(j))
        def _():
            fetch(j).start()

        return carry

    def forward(j, carry):
        @pl.when(is_near(j))
        def _():
            fetch(j).wait()
            pltpu.make_async_copy(held.at[j], out_ref.at[j], out_sem.at[j]).start()

        return carry

    def finish(j, carry):
        @pl.when((table_ref[j] < 0) | is_near(j))
        def _():
            pltpu.make_async_copy(zero, out_ref.at[j], out_sem.at[j]).wait()

        return carry

    lax.fori_loop(0, slots, start, 0)
    lax.fori_loop(0, slots, forward, 0)
    lax.fori_loop(0, slots, finish, 0)


def begin_output(table, split, near_spill):
    slots = table.shape[0]
    return pl.pallas_call(
        functools.partial(begin_kernel, split),
        out_shape=jax.ShapeDtypeStruct((slots, TILE, TILE), jnp.bfloat16),
        in_specs=[SMEM, HBM],
        out_specs=HBM,
        scratch_shapes=[
            pltpu.VMEM((TILE, TILE), jnp.bfloat16),
            pltpu.VMEM((slots, TILE, TILE), jnp.bfloat16),
            pltpu.SemaphoreType.DMA((slots,)),
            pltpu.SemaphoreType.DMA((slots,)),
        ],
        compiler_params=pltpu.CompilerParams(vmem_limit_bytes=55 * 1024 * 1024),
        cost_estimate=pl.CostEstimate(flops=0, bytes_accessed=8 * 1024 * 1024, transcendentals=0),
        name="begin_output",
    )(table, near_spill)


def place_kernel(split, far_from, table_ref, begun_ref, direct_ref, far_ref, out_ref, held, in_sem, out_sem):
    slots = out_ref.shape[0]

    def is_direct(j):
        return (table_ref[j] >= 0) & (table_ref[j] < split)

    def fetch(ref, place, j):
        return pltpu.make_async_copy(ref.at[place], held.at[j], in_sem.at[j])

    def store(j):
        return pltpu.make_async_copy(held.at[j], out_ref.at[j], out_sem.at[j])

    def begin(j, carry):
        source = table_ref[j]

        @pl.when(is_direct(j))
        def _():
            fetch(direct_ref, source, j).start()

        @pl.when(source >= far_from)
        def _():
            fetch(far_ref, source - far_from, j).start()

        return carry

    def forward(j, carry):
        @pl.when(is_direct(j) | (table_ref[j] >= far_from))
        def _():
            fetch(direct_ref, 0, j).wait()
            store(j).start()

        return carry

    def finish(j, carry):
        @pl.when(is_direct(j) | (table_ref[j] >= far_from))
        def _():
            store(j).wait()

        return carry

    lax.fori_loop(0, slots, begin, 0)
    lax.fori_loop(0, slots, forward, 0)
    lax.fori_loop(0, slots, finish, 0)


def place_tiles(table, begun, direct, far_from, far_spill):
    slots = table.shape[0]
    return pl.pallas_call(
        functools.partial(place_kernel, direct.shape[0], far_from),
        out_shape=jax.ShapeDtypeStruct((slots, TILE, TILE), jnp.bfloat16),
        in_specs=[SMEM, HBM, HBM, HBM],
        out_specs=HBM,
        scratch_shapes=[
            pltpu.VMEM((slots, TILE, TILE), jnp.bfloat16),
            pltpu.SemaphoreType.DMA((slots,)),
            pltpu.SemaphoreType.DMA((slots,)),
        ],
        input_output_aliases={1: 0},
        compiler_params=pltpu.CompilerParams(vmem_limit_bytes=55 * 1024 * 1024),
        name="place_tiles",
    )(table, begun, direct, far_spill)


def exchange(tiles, ranks):
    count = tiles.shape[0] // ranks
    sent = tiles.reshape(ranks, count, TILE, TILE)
    return lax.all_to_all(sent, "row", split_axis=0, concat_axis=0, tiled=True).reshape(
        ranks * count, TILE, TILE
    )


def local(t2_panels, t2_mask, v_blocks, v_mask, r_mask, owner_map, section_owner):
    ranks = lax.axis_size("row")
    me = lax.axis_index("row")
    slots_each = max(2, 2 * TILES // ranks)
    direct = slots_each // 2
    top = ranks // 2
    roots = section_owner

    own, give, short_places, long_places, spill_tiles, spill_goes = prepare(
        t2_panels,
        me.reshape(1),
        t2_mask,
        owner_map[:, :, 0].T,
        r_mask,
        ranks,
        slots_each,
        direct,
    )
    v = v_blocks.reshape(SECTIONS * KPT * TILE, NT_DEV * TILE)
    columns = fetch_columns(v, spill_tiles)

    def digest(notes, xors):
        notes = notes[:, : TILES + MT * KPT + 2].astype(jnp.int32)
        devices = me ^ jnp.asarray(xors, jnp.int32)
        order = jnp.arange(ranks, dtype=jnp.int32)
        root_rows = jnp.sum(jnp.where(devices[None, :] == roots[:, None], order, 0), axis=1)
        pairs, at, most = pair_up(me.reshape(1), root_rows, notes)
        return most, notes, devices, pairs, at, columns

    mine, got, worst, facts = spread(own, give, me, roots, ranks, digest)
    notes, devices, pairs, at, columns = facts
    mine, got = mine.reshape(-1, TILE), got.reshape(-1, TILE)

    split = ranks * direct

    def table_of(notes, far_each):
        owners, keep = notes[:, :TILES] // 2, notes[:, :TILES] % 2 != 0
        device = devices[:, None]
        rank, kept_rank, spills, spill_place = ranks_of(owners, keep, ((owners ^ device) & top) != 0, direct)
        slot = jnp.arange(slots_each, dtype=jnp.int32)
        if far_each:
            member = device & (top - 1)
            from_near = split + member * SPILL + spill_place
            from_far = split + (top * SPILL) + member * far_each + spill_place
            spilled_from = jnp.where(((device ^ me) & top) != 0, from_far, from_near)
            origin = jnp.where(spills, spilled_from, device * direct + kept_rank)
        else:
            origin = device * slots_each + kept_rank
        arrives = ((owners == me) & keep)[:, None, :] & (rank[:, None, :] == slot[None, :, None])
        listed = jnp.sum(jnp.where(arrives, origin[:, None, :] + 1, 0), axis=2)
        in_place = devices[None, :] == jnp.arange(ranks, dtype=jnp.int32)[:, None]
        return (jnp.sum(jnp.where(in_place[:, :, None], listed[None], 0), axis=1) - 1).reshape(-1)

    halves = [list(range(top)), list(range(top, ranks))]

    def gathered(spill):
        return lax.all_gather(spill, "row", axis=0, tiled=True, axis_index_groups=halves)

    def short(far_each, mine, got, v, v_mask, columns, notes, spill_tiles, spill_goes, places, _):
        near, far = spilled(far_each, mine, got, at, columns, v_mask, spill_tiles, spill_goes)
        near_spill = gathered(near)
        far = swap(far, top, ranks)
        tiles = ladder(mine, got, pairs, v, v_mask, places, split)
        far, tiles, notes = lax.optimization_barrier((far, tiles, notes))
        far_spill = gathered(far)
        table = table_of(notes, far_each)
        begun = begin_output(table, split, near_spill)
        return place_tiles(table, begun, exchange(tiles, ranks), split + top * SPILL, far_spill)

    def long(mine, got, v, v_mask, _, notes, __, ___, ____, places):
        tiles = ladder(mine, got, pairs, v, v_mask, places, ranks * slots_each)
        unused = jnp.zeros((1, TILE, TILE), jnp.bfloat16)
        table = table_of(notes, 0)
        begun = begin_output(table, ranks * slots_each, unused)
        return place_tiles(table, begun, exchange(tiles, ranks), ranks * slots_each + 1, unused)

    way = jnp.where(worst[0, 0] > SPILL, 2, (worst[0, 1] == SPILL).astype(jnp.int32))
    delivered = lax.switch(
        way,
        [functools.partial(short, SPILL - 1), functools.partial(short, SPILL), long],
        mine,
        got,
        v,
        v_mask,
        columns,
        notes,
        spill_tiles,
        spill_goes,
        short_places,
        long_places,
    )
    return delivered.reshape(ranks, slots_each, TILE, TILE)


def solution(mesh):
    placed = (
        P(("groups", "row"), None, None),
        P(("groups", "row"), None, None),
        P("groups", None, "row"),
        P("groups", None, "row"),
        P("groups", "row"),
        P(("groups", "row"), None, None),
        P("groups"),
    )
    return jax.shard_map(
        local,
        mesh=mesh,
        in_specs=placed,
        out_specs=P(("groups", "row"), None, None, None),
        check_vma=False,
    )
```

```python
import functools

import jax
import jax.numpy as jnp
from jax import lax
from jax.experimental import pallas as pl
from jax.experimental.pallas import tpu as pltpu
from jax.sharding import PartitionSpec as P

TILE = 256
MT = 4
KPT = 5
NT_DEV = 8
SECTIONS = 2
PCAP = 10
TILES = MT * NT_DEV
SPILL = 3
SPILL_TERMS = 4
STEP_TILES = 2
STEP_COLS = STEP_TILES * TILE
PAIRS = (SECTIONS * PCAP + MT) // 2
ANY = pl.BlockSpec(memory_space=pl.ANY)
HBM = pl.BlockSpec(memory_space=pltpu.HBM)
SMEM = pl.BlockSpec(memory_space=pltpu.SMEM)
VMEM = pl.BlockSpec(memory_space=pltpu.VMEM)


def swap(x, bit, ranks):
    return lax.ppermute(x, "row", [(i, i ^ bit) for i in range(ranks)])


def swap_with(x, note, bit, ranks):
    rows = x.shape[0] * x.shape[1]
    got = swap(jnp.concatenate([x.reshape(rows, -1), note], axis=0), bit, ranks)
    return got[:rows].reshape(x.shape), got[rows:]


def near(me, roots, bit):
    return (((me ^ roots) & bit) == 0)[:, None, None]


def scatter_step(x, note, me, roots, bit, ranks):
    half = x.shape[1] // 2
    high = (me & bit) != 0
    low_rows, high_rows = x[:, :half], x[:, half:]
    own, give = jnp.where(high, high_rows, low_rows), jnp.where(high, low_rows, high_rows)
    if note is None:
        got = swap(give, bit, ranks)
    else:
        got, note = swap_with(give, note, bit, ranks)
    return jnp.where(near(me, roots, bit), own, got), note


def middle_step(x, me, roots, bit, ranks):
    return jnp.where(near(me, roots, bit), x, swap(x, bit, ranks))


def gather_step(x, me, bit, ranks):
    got, high = swap(x, bit, ranks), (me & bit) != 0
    return jnp.concatenate([jnp.where(high, got, x), jnp.where(high, x, got)], axis=1)


def most_of_groups(most):
    groups = lax.axis_size("groups")
    worst = most
    for turn in range(1, groups):
        worst = jnp.maximum(
            worst, lax.ppermute(most, "groups", [(g, (g + turn) % groups) for g in range(groups)])
        )
    return worst


def spread(own, give, me, roots, ranks, digest):
    rows = own.shape[0]
    got = swap(give, 1, ranks)
    note, xors = jnp.concatenate([give[rows : rows + 1], got[rows : rows + 1]], axis=0), [0, 1]
    half, same = rows // 2, near(me, roots, 1)
    a = jnp.where(same, own[None, :half], got[None, :half])
    b = jnp.where(same, own[None, half:], got[None, half:rows])
    a, got_note = scatter_step(a, note, me, roots, 2, ranks)
    b, _ = scatter_step(b, None, me, roots, 4, ranks)
    across, across_xors, bit = note, xors, 8
    while bit < ranks:
        across = jnp.concatenate([across, swap(across, bit, ranks)], axis=0)
        across_xors = across_xors + [i ^ bit for i in across_xors]
        bit *= 2
    note, xors = jnp.concatenate([across, got_note], axis=0), across_xors + [2, 3]
    a, got_note = scatter_step(a, note, me, roots, 4, ranks)
    b, _ = scatter_step(b, None, me, roots, 2, ranks)
    note, xors = jnp.concatenate([note, got_note], axis=0), xors + [i ^ 4 for i in xors]
    missing = [i for i, other in enumerate(xors) if other >= 8]
    if missing:
        sent = jnp.concatenate([note[i : i + 1] for i in missing], axis=0)
        note = jnp.concatenate([note, swap(sent, 2, ranks)], axis=0)
        xors = xors + [xors[i] ^ 2 for i in missing]
    facts = digest(note, xors)
    worst = most_of_groups(facts[0])
    bit = 8
    while bit < ranks:
        a, b = middle_step(a, me, roots, bit, ranks), middle_step(b, me, roots, bit, ranks)
        bit *= 2
    a, b, worst, facts = lax.optimization_barrier((a, b, worst, facts))
    a, b = gather_step(a, me, 4, ranks), gather_step(b, me, 2, ranks)
    a, b = gather_step(a, me, 2, ranks), gather_step(b, me, 4, ranks)
    mine = jnp.concatenate([a, b], axis=1)
    return mine, swap(mine, 1, ranks), worst, facts[1:]


def ranks_of(owners, keep, far, direct):
    order = jnp.arange(TILES)
    earlier = order[None, :] < order[:, None]
    same = (owners[:, :, None] == owners[:, None, :]) & earlier
    rank = jnp.sum(same, axis=2, dtype=jnp.int32)
    kept_rank = jnp.sum(same & keep[:, None, :], axis=2, dtype=jnp.int32)
    spills = keep & (kept_rank >= direct)
    alike = (far[:, :, None] == far[:, None, :]) & earlier
    spill_place = jnp.sum(spills[:, None, :] & alike, axis=2, dtype=jnp.int32)
    return rank, kept_rank, spills, spill_place


def prepare_kernel(
    slots_each, direct, me_ref, mask_ref, owner_ref, keep_ref, panel_ref,
    own_ref, give_ref, short_ref, long_ref, spill_ref, goes_ref, kept, sem,
):
    half = PCAP // 2
    high = me_ref[0] % 2

    def tile_copy(place, ref, row, number):
        m, k = place // KPT, place % KPT
        return pltpu.make_async_copy(
            panel_ref.at[0, m * TILE : (m + 1) * TILE, k * TILE : (k + 1) * TILE],
            ref.at[pl.ds(pl.multiple_of(row * TILE, TILE), TILE)],
            sem.at[number],
        )

    number = jnp.int32(0)
    for place in range(MT * KPT):
        here = mask_ref[0, place // KPT, place % KPT] != 0
        upper = (number >= half).astype(jnp.int32)
        row = jnp.minimum(number - upper * half, half - 1)
        slot = jnp.minimum(number, PCAP - 1)

        @pl.when(here & (upper == high))
        def _(place=place, row=row, slot=slot):
            tile_copy(place, own_ref, row, slot).start()

        @pl.when(here & (upper != high))
        def _(place=place, row=row, slot=slot):
            tile_copy(place, give_ref, row, slot).start()

        number = number + here.astype(jnp.int32)

    column = lax.broadcasted_iota(jnp.int32, (16, TILE), 1)
    note = jnp.zeros((16, TILE), jnp.float32)
    for place in range(MT * KPT):
        note = jnp.where(column == TILES + place, mask_ref[0, place // KPT, place % KPT].astype(jnp.float32), note)
    for e in range(SPILL):
        spill_ref[e] = -1
        goes_ref[e] = -1
    for o in range(kept.shape[0]):
        kept[o] = 0
    near_count, far_count = jnp.int32(0), jnp.int32(0)
    top = kept.shape[0] // 2
    for q in range(TILES):
        owner = owner_ref[q % MT, q // MT]
        keep = (keep_ref[q % MT, q // MT] != 0).astype(jnp.int32)
        rank = kept[owner]
        kept[owner] = rank + keep
        over = keep * (rank >= direct).astype(jnp.int32)
        short_ref[q] = jnp.where(keep * (1 - over) != 0, owner * direct + rank, -1)
        long_ref[q] = jnp.where(keep != 0, owner * slots_each + rank, -1)

        far = (owner // top != me_ref[0] // top).astype(jnp.int32) * over
        near = over - far

        count = near_count + far_count

        @pl.when((over != 0) & (count < SPILL))
        def _(q=q, count=count, goes=jnp.where(far != 0, SPILL + far_count, near_count)):
            spill_ref[jnp.minimum(count, SPILL - 1)] = q
            goes_ref[jnp.minimum(count, SPILL - 1)] = goes

        far_count, near_count = far_count + far, near_count + near
        note = jnp.where(column == q, (owner * 2 + keep).astype(jnp.float32), note)
    note = jnp.where(column == TILES + MT * KPT, (near_count + far_count).astype(jnp.float32), note)
    note = jnp.where(column == TILES + MT * KPT + 1, far_count.astype(jnp.float32), note)
    give_ref[half * TILE : half * TILE + 16, :] = note.astype(jnp.bfloat16)
    for number in range(PCAP):
        tile_copy(0, own_ref, 0, number).wait()


def prepare(panel, me, mask, owners, keep, ranks, slots_each, direct):
    rows = PCAP // 2 * TILE
    places = jax.ShapeDtypeStruct((TILES,), jnp.int32)
    return pl.pallas_call(
        functools.partial(prepare_kernel, slots_each, direct),
        out_shape=(
            jax.ShapeDtypeStruct((rows, TILE), jnp.bfloat16),
            jax.ShapeDtypeStruct((rows + 16, TILE), jnp.bfloat16),
            places,
            places,
            jax.ShapeDtypeStruct((SPILL,), jnp.int32),
            jax.ShapeDtypeStruct((SPILL,), jnp.int32),
        ),
        in_specs=[SMEM, SMEM, SMEM, SMEM, ANY],
        out_specs=(VMEM, VMEM, SMEM, SMEM, SMEM, SMEM),
        scratch_shapes=[pltpu.SMEM((ranks,), jnp.int32), pltpu.SemaphoreType.DMA((PCAP,))],
        compiler_params=pltpu.CompilerParams(vmem_limit_bytes=62 * 1024 * 1024),
        name="prepare",
    )(me, mask, owners, keep, panel)


def pair_kernel(me_ref, root_row_ref, note_ref, row_ref, panel_tile_ref, v_tile_ref, at_ref, most_ref):
    def listed(s, place):
        return (note_ref[root_row_ref[s], TILES + place] != 0).astype(jnp.int32)

    for kind in range(2):
        most = jnp.int32(0)
        for device in range(note_ref.shape[0]):
            most = jnp.maximum(most, note_ref[device, TILES + MT * KPT + kind])
        most_ref[0, kind] = most
    for i in range(2 * PAIRS):
        panel_tile_ref[i] = 0
        v_tile_ref[i] = SECTIONS * KPT
    for pair in range(PAIRS):
        row_ref[pair] = MT - 1
    number = [jnp.int32(0)] * SECTIONS
    place_in_pairs = jnp.int32(0)
    for m in range(MT):
        for s in range(SECTIONS):
            for k in range(KPT):
                here = listed(s, m * KPT + k)
                upper = (number[s] >= PCAP // 2).astype(jnp.int32)
                away = (upper != me_ref[0] % 2).astype(jnp.int32)
                tile = 2 * (s * (PCAP // 2) + number[s] - upper * (PCAP // 2)) + away

                at_ref[(m * SECTIONS + s) * KPT + k] = jnp.where(here != 0, tile, -1)

                @pl.when(here != 0)
                def _(place_in_pairs=place_in_pairs, tile=tile, v_tile=s * KPT + k, m=m):
                    panel_tile_ref[place_in_pairs] = tile
                    v_tile_ref[place_in_pairs] = v_tile
                    row_ref[place_in_pairs // 2] = m

                place_in_pairs = place_in_pairs + here
                number[s] = number[s] + here
        place_in_pairs = (place_in_pairs + 1) // 2 * 2


def pair_up(me, root_rows, notes):
    members = jax.ShapeDtypeStruct((2 * PAIRS,), jnp.int32)
    *pairs, at, most = pl.pallas_call(
        pair_kernel,
        out_shape=(
            jax.ShapeDtypeStruct((PAIRS,), jnp.int32),
            members,
            members,
            jax.ShapeDtypeStruct((MT * SECTIONS * KPT,), jnp.int32),
            jax.ShapeDtypeStruct((1, 2), jnp.int32),
        ),
        in_specs=[SMEM, SMEM, SMEM],
        out_specs=(SMEM,) * 5,
        compiler_params=pltpu.CompilerParams(vmem_limit_bytes=4 * 1024 * 1024),
        cost_estimate=pl.CostEstimate(flops=0, bytes_accessed=8 * 1024 * 1024, transcendentals=0),
        name="pair_up",
    )(me, root_rows, notes)
    return pairs, at, most


def panel_at(panel_tile, mine_ref, got_ref):
    rows = pl.ds(pl.multiple_of(panel_tile // 2 * TILE, TILE), TILE)
    return jnp.where(panel_tile % 2 == 0, mine_ref[rows, :], got_ref[rows, :])


def pair_product(pair, panel_tile_ref, v_tile_ref, mine_ref, got_ref, v_ref, v_mask_ref, first_column):
    left, right = [], []
    tile_of = lax.broadcasted_iota(jnp.int32, (1, STEP_COLS), 1) // TILE
    for i in (2 * pair, 2 * pair + 1):
        v_tile = v_tile_ref[i]
        left.append(panel_at(panel_tile_ref[i], mine_ref, got_ref))
        v_row = jnp.minimum(v_tile, SECTIONS * KPT - 1)
        mask = jnp.zeros((1, STEP_COLS), jnp.float32)
        for j in range(STEP_TILES):
            kept = (v_mask_ref[v_row // KPT, lax.rem(v_row, KPT), first_column + j] != 0) & (v_row == v_tile)
            mask = jnp.where(tile_of == j, kept.astype(jnp.float32), mask)
        right.append(v_ref[pl.ds(pl.multiple_of(v_row * TILE, TILE), TILE), :] * mask.astype(jnp.bfloat16))
    return jnp.dot(
        jnp.concatenate(left, axis=1), jnp.concatenate(right, axis=0), preferred_element_type=jnp.float32
    )


def ladder_kernel(
    row_ref, panel_tile_ref, v_tile_ref, place_ref, v_mask_ref, mine_ref, got_ref, v_ref, out_ref, acc, staged, sem
):
    step = pl.program_id(0)
    acc[...] = jnp.zeros_like(acc)
    for pair in range(PAIRS):
        acc[row_ref[pair]] += pair_product(
            pair, panel_tile_ref, v_tile_ref, mine_ref, got_ref, v_ref, v_mask_ref, step * STEP_TILES
        )

    def copy_to(q, place):
        return pltpu.make_async_copy(staged.at[q], out_ref.at[place], sem.at[q])

    for j in range(STEP_TILES):
        for m in range(MT):
            q = (step * STEP_TILES + j) * MT + m
            staged[q] = acc[m, :, j * TILE : (j + 1) * TILE].astype(jnp.bfloat16)

            @pl.when(place_ref[q] >= 0)
            def _():
                copy_to(q, place_ref[q]).start()

    @pl.when(step == NT_DEV // STEP_TILES - 1)
    def _():
        def finish(q, carry):
            @pl.when(place_ref[q] >= 0)
            def _():
                copy_to(q, 0).wait()

            return carry

        lax.fori_loop(0, TILES, finish, 0)


def ladder(mine, got, pairs, v, v_mask, places, slots):
    macs = 2 * PAIRS * TILE * TILE * NT_DEV * TILE
    return pl.pallas_call(
        ladder_kernel,
        out_shape=jax.ShapeDtypeStruct((slots, TILE, TILE), jnp.bfloat16),
        grid=(NT_DEV // STEP_TILES,),
        in_specs=[
            SMEM,
            SMEM,
            SMEM,
            SMEM,
            SMEM,
            VMEM,
            VMEM,
            pl.BlockSpec((SECTIONS * KPT * TILE, STEP_COLS), lambda j: (0, j)),
        ],
        out_specs=HBM,
        scratch_shapes=[
            pltpu.VMEM((MT, TILE, STEP_COLS), jnp.float32),
            pltpu.VMEM((TILES, TILE, TILE), jnp.bfloat16),
            pltpu.SemaphoreType.DMA((TILES,)),
        ],
        compiler_params=pltpu.CompilerParams(vmem_limit_bytes=55 * 1024 * 1024),
        cost_estimate=pl.CostEstimate(flops=4 * macs, bytes_accessed=24 * 1024 * 1024, transcendentals=0),
        name="ladder",
    )(*pairs, places, v_mask, mine, got, v)


def column_of(tile):
    return pl.ds(pl.multiple_of(jnp.maximum(tile, 0) // MT * TILE, TILE), TILE)


def fetch_kernel(tile_ref, v_ref, out_ref, sem):
    copies = [
        pltpu.make_async_copy(v_ref.at[:, column_of(tile_ref[e])], out_ref.at[e], sem.at[e]) for e in range(SPILL)
    ]
    for copy in copies:
        copy.start()
    for copy in copies:
        copy.wait()


def fetch_columns(v, tiles):
    return pl.pallas_call(
        fetch_kernel,
        out_shape=jax.ShapeDtypeStruct((SPILL, v.shape[0], TILE), jnp.bfloat16),
        in_specs=[SMEM, HBM],
        out_specs=VMEM,
        scratch_shapes=[pltpu.SemaphoreType.DMA((SPILL,))],
        compiler_params=pltpu.CompilerParams(vmem_limit_bytes=16 * 1024 * 1024),
        cost_estimate=pl.CostEstimate(flops=0, bytes_accessed=8 * 1024 * 1024, transcendentals=0),
        name="fetch_columns",
    )(tiles, v)


def spill_kernel(
    tile_ref, goes_ref, at_ref, v_mask_ref, mine_ref, got_ref, v_ref, near_ref, far_ref, acc, panel_tiles, v_tiles
):
    terms = SECTIONS * KPT
    counts = []
    for e in range(SPILL):
        tile = jnp.maximum(tile_ref[e], 0)
        count = jnp.int32(0)
        for i in range(terms):
            panel_tile = at_ref[lax.rem(tile, MT) * terms + i]
            panel_tiles[e * (terms + 1) + count] = panel_tile
            v_tiles[e * (terms + 1) + count] = i
            counted = (panel_tile >= 0) & (v_mask_ref[i // KPT, i % KPT, tile // MT] != 0)
            count = count + counted.astype(jnp.int32)
        counts.append(count)

    def product(e, first):
        left, right = [], []
        for j in range(first, min(first + SPILL_TERMS, terms)):
            used = j < counts[e]
            value = panel_at(jnp.where(used, panel_tiles[e * (terms + 1) + j], 0), mine_ref, got_ref)
            left.append(jnp.where(used, value, jnp.zeros_like(value)))
            v_row = jnp.where(used, v_tiles[e * (terms + 1) + j], 0)
            right.append(v_ref[e, pl.ds(pl.multiple_of(v_row * TILE, TILE), TILE), :])
        return jnp.dot(
            jnp.concatenate(left, axis=1), jnp.concatenate(right, axis=0), preferred_element_type=jnp.float32
        )

    for e in range(SPILL):
        acc[e] = product(e, 0)
    for e in range(SPILL):
        for first in range(SPILL_TERMS, terms, SPILL_TERMS):

            @pl.when((counts[e] > first) & (tile_ref[e] >= 0))
            def _(e=e, first=first):
                acc[e] += product(e, first)

        goes = goes_ref[e]

        @pl.when((goes >= 0) & (goes < SPILL))
        def _(e=e, goes=goes):
            near_ref[jnp.clip(goes, 0, SPILL - 1)] = acc[e].astype(jnp.bfloat16)

        @pl.when((goes >= SPILL) & (goes < SPILL + far_ref.shape[0]))
        def _(e=e, goes=goes):
            far_ref[jnp.clip(goes - SPILL, 0, far_ref.shape[0] - 1)] = acc[e].astype(jnp.bfloat16)


def spilled(far_each, mine, got, at, columns, v_mask, tiles, goes):
    terms = SECTIONS * KPT
    return pl.pallas_call(
        spill_kernel,
        out_shape=(
            jax.ShapeDtypeStruct((SPILL, TILE, TILE), jnp.bfloat16),
            jax.ShapeDtypeStruct((far_each, TILE, TILE), jnp.bfloat16),
        ),
        in_specs=[SMEM] * 4 + [VMEM] * 3,
        out_specs=(VMEM, VMEM),
        scratch_shapes=[
            pltpu.VMEM((SPILL, TILE, TILE), jnp.float32),
            pltpu.SMEM((SPILL * (terms + 1),), jnp.int32),
            pltpu.SMEM((SPILL * (terms + 1),), jnp.int32),
        ],
        compiler_params=pltpu.CompilerParams(vmem_limit_bytes=24 * 1024 * 1024),
        name="spilled",
    )(tiles, goes, at, v_mask, mine, got, columns)


def begin_kernel(split, table_ref, near_ref, out_ref, zero, held, in_sem, out_sem):
    zero[...] = jnp.zeros_like(zero)
    slots, reach = out_ref.shape[0], near_ref.shape[0]

    def is_near(j):
        return (table_ref[j] >= split) & (table_ref[j] < split + reach)

    def fetch(j):
        return pltpu.make_async_copy(near_ref.at[jnp.maximum(table_ref[j] - split, 0)], held.at[j], in_sem.at[j])

    def start(j, carry):
        @pl.when(table_ref[j] < 0)
        def _():
            pltpu.make_async_copy(zero, out_ref.at[j], out_sem.at[j]).start()

        @pl.when(is_near(j))
        def _():
            fetch(j).start()

        return carry

    def forward(j, carry):
        @pl.when(is_near(j))
        def _():
            fetch(j).wait()
            pltpu.make_async_copy(held.at[j], out_ref.at[j], out_sem.at[j]).start()

        return carry

    def finish(j, carry):
        @pl.when((table_ref[j] < 0) | is_near(j))
        def _():
            pltpu.make_async_copy(zero, out_ref.at[j], out_sem.at[j]).wait()

        return carry

    lax.fori_loop(0, slots, start, 0)
    lax.fori_loop(0, slots, forward, 0)
    lax.fori_loop(0, slots, finish, 0)


def begin_output(table, split, near_spill):
    slots = table.shape[0]
    return pl.pallas_call(
        functools.partial(begin_kernel, split),
        out_shape=jax.ShapeDtypeStruct((slots, TILE, TILE), jnp.bfloat16),
        in_specs=[SMEM, HBM],
        out_specs=HBM,
        scratch_shapes=[
            pltpu.VMEM((TILE, TILE), jnp.bfloat16),
            pltpu.VMEM((slots, TILE, TILE), jnp.bfloat16),
            pltpu.SemaphoreType.DMA((slots,)),
            pltpu.SemaphoreType.DMA((slots,)),
        ],
        compiler_params=pltpu.CompilerParams(vmem_limit_bytes=55 * 1024 * 1024),
        cost_estimate=pl.CostEstimate(flops=0, bytes_accessed=8 * 1024 * 1024, transcendentals=0),
        name="begin_output",
    )(table, near_spill)


def place_kernel(split, far_from, table_ref, begun_ref, direct_ref, far_ref, out_ref, held, in_sem, out_sem):
    slots = out_ref.shape[0]

    def is_direct(j):
        return (table_ref[j] >= 0) & (table_ref[j] < split)

    def fetch(ref, place, j):
        return pltpu.make_async_copy(ref.at[place], held.at[j], in_sem.at[j])

    def store(j):
        return pltpu.make_async_copy(held.at[j], out_ref.at[j], out_sem.at[j])

    def begin(j, carry):
        source = table_ref[j]

        @pl.when(is_direct(j))
        def _():
            fetch(direct_ref, source, j).start()

        @pl.when(source >= far_from)
        def _():
            fetch(far_ref, source - far_from, j).start()

        return carry

    def forward(j, carry):
        @pl.when(is_direct(j) | (table_ref[j] >= far_from))
        def _():
            fetch(direct_ref, 0, j).wait()
            store(j).start()

        return carry

    def finish(j, carry):
        @pl.when(is_direct(j) | (table_ref[j] >= far_from))
        def _():
            store(j).wait()

        return carry

    lax.fori_loop(0, slots, begin, 0)
    lax.fori_loop(0, slots, forward, 0)
    lax.fori_loop(0, slots, finish, 0)


def place_tiles(table, begun, direct, far_from, far_spill):
    slots = table.shape[0]
    return pl.pallas_call(
        functools.partial(place_kernel, direct.shape[0], far_from),
        out_shape=jax.ShapeDtypeStruct((slots, TILE, TILE), jnp.bfloat16),
        in_specs=[SMEM, HBM, HBM, HBM],
        out_specs=HBM,
        scratch_shapes=[
            pltpu.VMEM((slots, TILE, TILE), jnp.bfloat16),
            pltpu.SemaphoreType.DMA((slots,)),
            pltpu.SemaphoreType.DMA((slots,)),
        ],
        input_output_aliases={1: 0},
        compiler_params=pltpu.CompilerParams(vmem_limit_bytes=55 * 1024 * 1024),
        name="place_tiles",
    )(table, begun, direct, far_spill)


def exchange(tiles, ranks):
    count = tiles.shape[0] // ranks
    sent = tiles.reshape(ranks, count, TILE, TILE)
    return lax.all_to_all(sent, "row", split_axis=0, concat_axis=0, tiled=True).reshape(
        ranks * count, TILE, TILE
    )


def local(t2_panels, t2_mask, v_blocks, v_mask, r_mask, owner_map, section_owner):
    ranks = lax.axis_size("row")
    me = lax.axis_index("row")
    slots_each = max(2, 2 * TILES // ranks)
    direct = slots_each // 2
    top = ranks // 2
    roots = section_owner

    own, give, short_places, long_places, spill_tiles, spill_goes = prepare(
        t2_panels,
        me.reshape(1),
        t2_mask,
        owner_map[:, :, 0].T,
        r_mask,
        ranks,
        slots_each,
        direct,
    )
    v = v_blocks.reshape(SECTIONS * KPT * TILE, NT_DEV * TILE)
    columns = fetch_columns(v, spill_tiles)

    def digest(notes, xors):
        notes = notes[:, : TILES + MT * KPT + 2].astype(jnp.int32)
        devices = me ^ jnp.asarray(xors, jnp.int32)
        order = jnp.arange(ranks, dtype=jnp.int32)
        root_rows = jnp.sum(jnp.where(devices[None, :] == roots[:, None], order, 0), axis=1)
        pairs, at, most = pair_up(me.reshape(1), root_rows, notes)
        return most, notes, devices, pairs, at, columns

    mine, got, worst, facts = spread(own, give, me, roots, ranks, digest)
    notes, devices, pairs, at, columns = facts
    mine, got = mine.reshape(-1, TILE), got.reshape(-1, TILE)

    split = ranks * direct

    def table_of(notes, far_each):
        owners, keep = notes[:, :TILES] // 2, notes[:, :TILES] % 2 != 0
        device = devices[:, None]
        rank, kept_rank, spills, spill_place = ranks_of(owners, keep, ((owners ^ device) & top) != 0, direct)
        slot = jnp.arange(slots_each, dtype=jnp.int32)
        if far_each:
            member = device & (top - 1)
            from_near = split + member * SPILL + spill_place
            from_far = split + (top * SPILL) + member * far_each + spill_place
            spilled_from = jnp.where(((device ^ me) & top) != 0, from_far, from_near)
            origin = jnp.where(spills, spilled_from, device * direct + kept_rank)
        else:
            origin = device * slots_each + kept_rank
        arrives = ((owners == me) & keep)[:, None, :] & (rank[:, None, :] == slot[None, :, None])
        listed = jnp.sum(jnp.where(arrives, origin[:, None, :] + 1, 0), axis=2)
        in_place = devices[None, :] == jnp.arange(ranks, dtype=jnp.int32)[:, None]
        return (jnp.sum(jnp.where(in_place[:, :, None], listed[None], 0), axis=1) - 1).reshape(-1)

    halves = [list(range(top)), list(range(top, ranks))]

    def gathered(spill):
        return lax.all_gather(spill, "row", axis=0, tiled=True, axis_index_groups=halves)

    def short(far_each, mine, got, v, v_mask, columns, notes, spill_tiles, spill_goes, places, _):
        near, far = spilled(far_each, mine, got, at, columns, v_mask, spill_tiles, spill_goes)
        near_spill = gathered(near)
        far = swap(far, top, ranks)
        tiles = ladder(mine, got, pairs, v, v_mask, places, split)
        far, tiles, notes = lax.optimization_barrier((far, tiles, notes))
        far_spill = gathered(far)
        table = table_of(notes, far_each)
        begun = begin_output(table, split, near_spill)
        return place_tiles(table, begun, exchange(tiles, ranks), split + top * SPILL, far_spill)

    def long(mine, got, v, v_mask, _, notes, __, ___, ____, places):
        tiles = ladder(mine, got, pairs, v, v_mask, places, ranks * slots_each)
        unused = jnp.zeros((1, TILE, TILE), jnp.bfloat16)
        table = table_of(notes, 0)
        begun = begin_output(table, ranks * slots_each, unused)
        return place_tiles(table, begun, exchange(tiles, ranks), ranks * slots_each + 1, unused)

    way = jnp.where(worst[0, 0] > SPILL, 2, (worst[0, 1] == SPILL).astype(jnp.int32))
    delivered = lax.switch(
        way,
        [functools.partial(short, SPILL - 1), functools.partial(short, SPILL), long],
        mine,
        got,
        v,
        v_mask,
        columns,
        notes,
        spill_tiles,
        spill_goes,
        short_places,
        long_places,
    )
    return delivered.reshape(ranks, slots_each, TILE, TILE)


def solution(mesh):
    placed = (
        P(("groups", "row"), None, None),
        P(("groups", "row"), None, None),
        P("groups", None, "row"),
        P("groups", None, "row"),
        P("groups", "row"),
        P(("groups", "row"), None, None),
        P("groups"),
    )
    return jax.shard_map(
        local,
        mesh=mesh,
        in_specs=placed,
        out_specs=P(("groups", "row"), None, None, None),
        check_vma=False,
    )
```
